128 devices in a mesh: bx: 8 (over y, core), by: 16 (over x, z).
Axes of the slice: x: 4, y: 4, z: 4, core: 2. Of those that a mesh axis runs over, the one named last changes fastest.
Arguments:
- h_old: float32 [20, 512, 2048], P(None, 'bx', 'by'), may hold values from -3 to 0.5
- soil_type: int32 [20, 512, 2048], P(None, 'bx', 'by'), may hold values from 0 to 11
- ks_scale: float32 [20, 512, 2048], P(None, 'bx', 'by'), may hold values from 0.3 to 3
- soil_table: float32 [4, 12], replicated, may hold values from 0.2 to 1
- clump_brick: int32 [1048576], P(('bx', 'by')), may hold values from -1 to 127, as said below
- clump_cell: int32 [1048576], P(('bx', 'by')), may hold values from -1 to 8191, as said below
- root_fraction: float32 [14, 1048576], P(None, ('bx', 'by')), may hold values from 0.05 to 0.3
- transpiration: float32 [1048576], P(('bx', 'by')), may hold values from 0.2 to 2
- infiltration: float32 [1048576], P(('bx', 'by')), may hold values from 0.2 to 2
Outputs:
- pressure: float32 [20, 512, 2048], P(None, 'bx', 'by')
- stress: float32 [1048576], P(('bx', 'by'))
The draws below stay inside these ranges and needn't reach their ends.
Inputs may be any that keep to these rules, and one draw needn't show every extreme that they name: `clump_brick`: A brick is the 64 x 128 columns with i // 64 and j // 128 fixed, numbered (i // 64) * 16 + j // 128. The slots of one device are the 8192 consecutive entries of its shard; its slots b * 64 to (b + 1) * 64 - 1 hold columns of brick b or are empty, and there the entry is b; -1 marks an empty slot (exactly where clump_cell is -1). `clump_cell`: A slot's entry is the position (i % 64) * 128 + j % 128 of its column within its brick, or -1 when empty; no column is held twice. In every draw one brick has all its columns held, all 64 of its slots filled on every device.
All inputs are finite; a program needn't handle non-finite values.
Results may differ from the reference program's by a relative error of at most 0.000068.
Values sent between devices are 32-bit elements; how exact they have to be, the bound alone decides.
A program may use at most 64 MiB of HBM per device.

```python
import math
import jax
import jax.numpy as jnp
from jax import lax

CX = 64
CY = 128
LAY = 20
ROOT = 14
ITERS = 2
NSOIL = 12
NXG = 512
NYG = 2048
COLUMNS = 1048576
N_BX = 8
N_BY = 16


def clump_layout(key):
    devices = N_BX * N_BY
    per_device = CX * CY
    per_peer = per_device // devices
    keys = jax.random.split(key, 5)
    levels = jax.random.randint(keys[0], (devices,), per_peer // 2 + 1, per_peer + 1)
    counts = jax.random.randint(keys[1], (devices, devices), 0, levels[None, :] + 1)
    busiest = jax.random.randint(keys[2], (), 0, devices)
    brick_ids = jnp.arange(devices, dtype=jnp.int32)
    counts = jnp.where(brick_ids[None, :] == busiest, per_peer, counts).astype(jnp.int32)
    offsets = jnp.cumsum(counts, axis=0) - counts
    spread = max(2, 2 ** 30 // per_device)
    scores = jax.random.randint(keys[3], (devices, per_device), 0, spread) * per_device + jnp.arange(per_device, dtype=jnp.int32)[None, :]
    perms = jnp.argsort(scores, axis=1).astype(jnp.int32)
    within = jnp.arange(per_peer, dtype=jnp.int32)
    used = within[None, None, :] < counts[:, :, None]
    where_in = jnp.minimum(offsets[:, :, None] + within[None, None, :], per_device - 1)
    local = perms[brick_ids[None, :, None], where_in]
    brick_full = jnp.broadcast_to(brick_ids[None, :, None], local.shape)
    cell_id = jnp.where(used, local, -1)
    brick_id = jnp.where(used, brick_full, -1)
    spread_peer = max(2, 2 ** 30 // per_peer)
    shuffle = jax.random.randint(keys[4], (devices, devices, per_peer), 0, spread_peer) * per_peer + within[None, None, :]
    order = jnp.argsort(shuffle, axis=2).astype(jnp.int32)
    cells = jnp.take_along_axis(cell_id, order, axis=2).reshape(-1).astype(jnp.int32)
    bricks = jnp.take_along_axis(brick_id, order, axis=2).reshape(-1).astype(jnp.int32)
    return (bricks, cells)


def draw_clump_brick(key, part):
    bricks, cells = clump_layout(jax.random.fold_in(key, 7))
    return bricks


def draw_clump_cell(key, part):
    bricks, cells = clump_layout(jax.random.fold_in(key, 7))
    return cells


def set_ends(array, stream_key, low, top_value):
    shape = array.shape
    place = [jax.random.randint(jax.random.fold_in(stream_key, axis), (), 0, shape[axis]) for axis in range(len(shape))]
    array = array.at[tuple(place)].set(low)
    longest = shape.index(max(shape))
    place[longest] = (place[longest] + 1) % shape[longest]
    return array.at[tuple(place)].set(top_value)


def block_scale(rng, shape, pieces, low, largest):
    loudness, own = 1.0, jax.random.fold_in(rng, 6)
    for position, blocks in pieces:
        heights = jnp.exp(jax.random.uniform(jax.random.fold_in(own, position), (blocks,), jnp.float32, low / len(pieces), largest / len(pieces)))
        loudness = loudness * jnp.repeat(heights, shape[position] // blocks).reshape([-1 if axis == position else 1 for axis in range(len(shape))])
    return loudness


def setup_inputs(seed: int = 0) -> dict:
    key_list = jax.random.split(jax.random.key(seed), 10)
    h_old = jnp.clip(-3.0 + 3.5 * jax.random.uniform(key_list[0], (LAY, NXG, NYG), jnp.float32) ** block_scale(key_list[0], (LAY, NXG, NYG), ((1, 8), (2, 16)), -0.2, 0.2), -3.0, 0.5)
    soil_type = set_ends(jax.random.randint(key_list[1], (LAY, NXG, NYG), 0, NSOIL), jax.random.fold_in(key_list[1], 1), 0, NSOIL - 1).astype(jnp.int32)
    ks_scale = jnp.clip(jnp.exp(math.log(3.0) - 2.3025851 * jax.random.uniform(key_list[2], (LAY, NXG, NYG), jnp.float32) ** block_scale(key_list[2], (LAY, NXG, NYG), ((1, 8), (2, 16)), -0.2, 0.2)), 0.3, 3.0)
    soil_table = jnp.clip(jax.random.uniform(key_list[3], (4, NSOIL), jnp.float32, 0.2, 1.0), 0.2, 1.0)
    clump_brick = draw_clump_brick(jax.random.fold_in(key_list[9], 71), 0)
    clump_cell = draw_clump_cell(jax.random.fold_in(key_list[9], 71), 0)
    root_fraction = jnp.clip(0.05 + 0.25 * jax.random.uniform(key_list[6], (ROOT, COLUMNS), jnp.float32) ** block_scale(key_list[6], (ROOT, COLUMNS), ((1, 128),), -0.2, 0.2), 0.05, 0.3)
    transpiration = jnp.clip(jnp.exp(math.log(2.0) - 2.3025851 * jax.random.uniform(key_list[7], (COLUMNS,), jnp.float32) ** block_scale(key_list[7], (COLUMNS,), ((0, 128),), -0.2, 0.2)), 0.2, 2.0)
    infiltration = jnp.clip(jnp.exp(math.log(2.0) - 2.3025851 * jax.random.uniform(key_list[8], (COLUMNS,), jnp.float32) ** block_scale(key_list[8], (COLUMNS,), ((0, 128),), -0.2, 0.2)), 0.2, 2.0)
    return {"h_old": h_old, "soil_type": soil_type, "ks_scale": ks_scale, "soil_table": soil_table, "clump_brick": clump_brick, "clump_cell": clump_cell, "root_fraction": root_fraction, "transpiration": transpiration, "infiltration": infiltration}


RESIDUAL_WATER = 0.05
STORAGE = 0.2
TIME_STEP = 0.5
LATERAL = 0.5

def closures(pressure, scale_alpha, shape_n, porosity, ksat):
    exponent = 1.0 - 1.0 / shape_n
    suction = scale_alpha * jnp.maximum(-pressure, 0.0)
    base_term = 1.0 + jnp.power(suction, shape_n)
    saturation = jnp.power(base_term, -exponent)
    moisture = RESIDUAL_WATER + (porosity - RESIDUAL_WATER) * saturation
    inner_term = 1.0 - jnp.power(1.0 - jnp.power(saturation, 1.0 / exponent), exponent)
    conduct = ksat * jnp.sqrt(saturation) * inner_term * inner_term
    storage = STORAGE + (porosity - RESIDUAL_WATER) * exponent * shape_n * scale_alpha * jnp.power(suction, shape_n - 1.0) * jnp.power(base_term, -exponent - 1.0)
    return (saturation, moisture, conduct, storage)

def thomas(diagonal, coupling, target):
    layers = diagonal.shape[0]
    ratios = []
    values = []
    pivot_value = diagonal[0]
    if layers > 1:
        ratios.append(coupling[0] / pivot_value)
    values.append(target[0] / pivot_value)
    for layer_index in range(1, layers):
        pivot_value = diagonal[layer_index] - coupling[layer_index - 1] * ratios[layer_index - 1]
        if layer_index < layers - 1:
            ratios.append(coupling[layer_index] / pivot_value)
        values.append((target[layer_index] - coupling[layer_index - 1] * values[layer_index - 1]) / pivot_value)
    result = [values[layers - 1]]
    for layer_index in range(layers - 2, -1, -1):
        result.insert(0, values[layer_index] - ratios[layer_index] * result[0])
    return jnp.stack(result)

def reference(h_old, soil_type, ks_scale, soil_table, clump_brick, clump_cell, root_fraction, transpiration, infiltration):
    params = jnp.take(soil_table, soil_type, axis=1)
    scale_alpha = 4.0 * params[0]
    shape_n = 1.2 + 2.0 * params[1]
    ksat = 3.0 * params[2] * ks_scale
    porosity = 0.3 + 0.3 * params[3]
    columns = NXG * NYG
    valid = clump_cell >= 0
    brick_safe = jnp.where(valid, clump_brick, 0).astype(jnp.int32)
    cell_safe = jnp.where(valid, clump_cell, 0).astype(jnp.int32)
    row_global = brick_safe // N_BY * CX + cell_safe // CY
    col_global = brick_safe % N_BY * CY + cell_safe % CY
    column_id = (row_global * NYG + col_global).astype(jnp.int32)
    target_index = jnp.where(valid, column_id, columns).astype(jnp.int32)
    forcing = jnp.concatenate([root_fraction, transpiration[None], infiltration[None]], 0)
    grid = jnp.zeros((ROOT + 2, columns), jnp.float32).at[:, target_index].set(forcing, mode='drop')
    grid = grid.reshape(ROOT + 2, NXG, NYG)
    sink = grid[ROOT][None] * grid[:ROOT]
    sink_full = jnp.concatenate([sink, jnp.zeros((LAY - ROOT, NXG, NYG), jnp.float32)], 0)
    inflow_top = grid[ROOT + 1]
    pressure = h_old
    saturation, moisture, conduct, storage = closures(pressure, scale_alpha, shape_n, porosity, ksat)
    moisture_old = moisture
    for step_index in range(ITERS):
        vert_k = 0.5 * (conduct[:-1] + conduct[1:])
        vert_flux = vert_k * (pressure[:-1] - pressure[1:] + 1.0)
        down_out = jnp.concatenate([vert_flux, conduct[-1:]], 0)
        from_above = jnp.concatenate([inflow_top[None], vert_flux], 0)
        face_x = 0.5 * (conduct[:, :-1] + conduct[:, 1:])
        flow_x = LATERAL * face_x * (pressure[:, :-1] - pressure[:, 1:])
        face_y = 0.5 * (conduct[:, :, :-1] + conduct[:, :, 1:])
        flow_y = LATERAL * face_y * (pressure[:, :, :-1] - pressure[:, :, 1:])
        pad_hi_x = ((0, 0), (0, 1), (0, 0))
        pad_lo_x = ((0, 0), (1, 0), (0, 0))
        pad_hi_y = ((0, 0), (0, 0), (0, 1))
        pad_lo_y = ((0, 0), (0, 0), (1, 0))
        lateral = jnp.pad(flow_x, pad_hi_x) - jnp.pad(flow_x, pad_lo_x) + (jnp.pad(flow_y, pad_hi_y) - jnp.pad(flow_y, pad_lo_y))
        residual = (moisture - moisture_old) / TIME_STEP + (down_out - from_above) + lateral + sink_full
        lateral_sum = jnp.pad(face_x, pad_hi_x) + jnp.pad(face_x, pad_lo_x) + (jnp.pad(face_y, pad_hi_y) + jnp.pad(face_y, pad_lo_y))
        diagonal = storage / TIME_STEP + jnp.pad(vert_k, ((1, 0), (0, 0), (0, 0))) + jnp.pad(vert_k, ((0, 1), (0, 0), (0, 0))) + LATERAL * lateral_sum
        delta = thomas(diagonal, -vert_k, -residual)
        pressure = pressure + delta
        saturation, moisture, conduct, storage = closures(pressure, scale_alpha, shape_n, porosity, ksat)
    root_state = saturation[:ROOT].reshape(ROOT, columns)
    safe_col = jnp.where(valid, column_id, 0).astype(jnp.int32)
    at_slot = root_state[:, safe_col]
    numer = lax.optimization_barrier(jnp.sum(root_fraction * at_slot, 0))
    denom = lax.optimization_barrier(jnp.sum(root_fraction, 0))
    stress = jnp.where(valid, numer / denom, 0.0)
    return (pressure, stress)
```

```python
import functools

import jax
import jax.numpy as jnp
from jax import lax
from jax.experimental import pallas as pl
from jax.experimental.pallas import tpu as pltpu
from jax.sharding import PartitionSpec as P

MESH = pl.DeviceIdType.MESH
NX, NY = 8, 16
PEERS = NX * NY
LAY, ROOT = 20, 14
RX, RY = 64, 128
SLOTS = RX * RY
FIELDS = ROOT + 1
BLOCK = 16
TINY = 1e-30
F32, BF16, I32 = jnp.float32, jnp.bfloat16, jnp.int32


def closures(head, alpha, shape_n, exponent, ks, width):
    log_s = shape_n * jnp.log2(alpha * jnp.maximum(-head, TINY))
    log_b = jnp.log2(1.0 + jnp.exp2(log_s))
    log_w = exponent * (log_s - log_b)
    root = jnp.exp2(-0.5 * exponent * log_b)
    inner = 1.0 - jnp.exp2(log_w)
    conduct = ks * root * (inner * inner)
    storage = 0.4 + 2.0 * width * (shape_n - 1.0) * alpha * jnp.exp2(log_w - log_b)
    return root, conduct, storage


def kernel(
    h_hbm, soil_hbm, ks_hbm, table_ref, cell_hbm, root_hbm, transp_hbm, infil_hbm,
    p_out, s_out,
    h, soil, ks_in, cell, root, transp, infil,
    table, fields1, send, recv,
    par_a, par_n, par_e, par_k, par_w,
    pk, sat_old, stor, lat, gsum,
    rinv, low, upp, rhs, val,
    a_mat, b_mat, row_of, acc, grid,
    ypack, yrecv, xrecv, ycomb,
    back, mine,
    in_sem, send_sem, recv_sem, halo_send, halo_recv, ret_send, ret_recv, out_sem,
):
    bx = lax.axis_index("bx")
    by = lax.axis_index("by")
    me = bx * NY + by

    copies = [
        pltpu.make_async_copy(src, dst, in_sem.at[i])
        for i, (src, dst) in enumerate(
            (
                (root_hbm, root), (transp_hbm, transp), (infil_hbm, infil), (cell_hbm, cell),
                (h_hbm, h), (soil_hbm, soil), (ks_hbm, ks_in),
            )
        )
    ]
    for copy in copies:
        copy.start()

    def peer(i):
        dx, dy = i // NY, lax.rem(i, NY)
        return lax.rem(bx + dx, NX), lax.rem(by + dy, NY)

    barrier = pltpu.get_barrier_semaphore()

    def greet(i, carry):
        pl.semaphore_signal(barrier, inc=1, device_id=peer(i), device_id_type=MESH)
        return carry

    lax.fori_loop(1, PEERS, greet, 0)

    lane8 = lax.broadcasted_iota(I32, (8, 128), 1)
    sub8 = lax.broadcasted_iota(I32, (8, 128), 0)
    first_half = lane8 < 64

    for copy in copies[:4]:
        copy.wait()
    fields1[0:6, :] = root[8:14, :]
    fields1[6:7, :] = infil[...]
    fields1[7:8, :] = cell[...].astype(F32)

    def pack(q, carry):
        at = pl.ds(pl.multiple_of(q * 128, 128), 128)
        demand = transp[:, at]
        v0 = root[0:8, at] * demand
        v1 = fields1[:, at] * jnp.where(sub8 < 6, demand, 1.0)
        r0 = pltpu.roll(v0, 64, 1)
        r1 = pltpu.roll(v1, 64, 1)
        send[2 * q] = jnp.where(first_half, v0, r1)
        send[2 * q + 1] = jnp.where(first_half, r0, v1)
        return carry

    lax.fori_loop(0, PEERS // 2, pack, 0)

    pl.semaphore_wait(barrier, PEERS - 1)

    own = pltpu.make_async_copy(send.at[me], recv.at[bx, by], recv_sem.at[bx])
    own.start()

    def push(i, carry):
        tx, ty = peer(i)
        pltpu.make_async_remote_copy(
            send.at[tx * NY + ty], recv.at[bx, by], send_sem, recv_sem.at[bx],
            device_id=(tx, ty), device_id_type=MESH,
        ).start()
        return carry

    lax.fori_loop(1, PEERS, push, 0)

    table[...] = jnp.zeros_like(table)
    table[0:4, 0:12] = table_ref[...]
    for copy in copies[4:]:
        copy.wait()
    t0, t1, t2, t3 = (jnp.broadcast_to(table[i : i + 1, :], (RX, 128)) for i in range(4))
    lane = lax.broadcasted_iota(I32, (RX, 128), 1)

    def first(k, packed):
        kind = soil[k]
        look = lambda t: jnp.take_along_axis(t, kind, axis=1, mode="promise_in_bounds")
        alpha = 4.0 * look(t0)
        shape_n = 1.2 + 2.0 * look(t1)
        ks = 0.75 * look(t2) * ks_in[k]
        width = 0.25 + 0.3 * look(t3)
        exponent = 1.0 - 1.0 / shape_n
        par_a[k], par_n[k], par_e[k], par_k[k], par_w[k] = alpha, shape_n, exponent, ks, width
        head = h[k]
        sq, conduct, storage = closures(head, alpha, shape_n, exponent, ks, width)
        sat_old[k] = sq * sq
        stor[k] = storage
        pk[0, k, 8 : 8 + RX, :] = head
        pk[1, k, 8 : 8 + RX, :] = conduct
        turn = 2 * k + 1
        pair = lane // 2
        packed = jnp.where(pair == k, pltpu.roll(head, turn, 1), packed)
        packed = jnp.where(pair == k + 32, pltpu.roll(conduct, turn + 64, 1), packed)
        return packed

    ypack[0] = lax.fori_loop(0, LAY, first, jnp.zeros((RX, 128), F32))

    def halo_copies(step):
        up = lax.rem(bx + NX - 1, NX), by
        down = lax.rem(bx + 1, NX), by
        left = bx, lax.rem(by + NY - 1, NY)
        right = bx, lax.rem(by + 1, NY)
        moves = (
            (pk.at[:, :, pl.ds(64, 8), :], xrecv.at[step, 0], down),
            (pk.at[:, :, pl.ds(8, 8), :], xrecv.at[step, 1], up),
            (ypack.at[step], yrecv.at[step, 0], right),
            (ypack.at[step], yrecv.at[step, 1], left),
        )
        return [
            pltpu.make_async_remote_copy(
                src, dst, halo_send.at[step, i], halo_recv.at[step, i],
                device_id=to, device_id_type=MESH,
            )
            for i, (src, dst, to) in enumerate(moves)
        ]

    odd = lax.rem(lane, 2) == 1

    def halo_finish(step, moves):
        for move in moves:
            move.wait_recv()
        for move in moves:
            move.wait_send()
        for k in range(LAY):
            pk[0, k, 7:8, :] = xrecv[step, 0, 0, k, 7:8, :]
            pk[0, k, 72:73, :] = xrecv[step, 1, 0, k, 0:1, :]
            pk[1, k, 7:8, :] = jnp.where(bx == 0, -pk[1, k, 8:9, :], xrecv[step, 0, 1, k, 7:8, :])
            pk[1, k, 72:73, :] = jnp.where(
                bx == NX - 1, -pk[1, k, 71:72, :], xrecv[step, 1, 1, k, 0:1, :]
            )
        both = jnp.where(
            odd, pltpu.roll(yrecv[step, 0], 1, 1), pltpu.roll(yrecv[step, 1], 127, 1)
        )
        edge = jnp.logical_or(
            jnp.logical_and(odd, by == 0), jnp.logical_and(jnp.logical_not(odd), by == NY - 1)
        )
        ycomb[...] = jnp.where(edge, -ypack[step], both)

    at_first, at_last = lane == 0, lane == 127

    def sideways(k, carry):
        head, conduct = pk[0, k, 8:72, :], pk[1, k, 8:72, :]
        comb = ycomb[...]
        hp = pltpu.roll(comb, 127 - 2 * k, 1)
        hk = pltpu.roll(comb, 63 - 2 * k, 1)
        left_p = jnp.where(at_first, hp, pltpu.roll(head, 1, 1))
        left_k = jnp.where(at_first, hk, pltpu.roll(conduct, 1, 1))
        right_p = jnp.where(at_last, hp, pltpu.roll(head, 127, 1))
        right_k = jnp.where(at_last, hk, pltpu.roll(conduct, 127, 1))
        gl, gr = conduct + left_k, conduct + right_k
        gu, gd = conduct + pk[1, k, 7:71, :], conduct + pk[1, k, 9:73, :]
        gsum[k] = (gl + gr) + (gu + gd)
        lat[k] = (gl * (head - left_p) + gr * (head - right_p)) + (
            gu * (head - pk[0, k, 7:71, :]) + gd * (head - pk[0, k, 9:73, :])
        )
        return carry

    moves = halo_copies(0)
    for move in moves:
        move.start()
    halo_finish(0, moves)
    lax.fori_loop(0, LAY, sideways, 0)

    def factor_first(r, carry):
        rows = pl.ds(pl.multiple_of(r * BLOCK, BLOCK), BLOCK)
        prow = pl.ds(pl.multiple_of(r * BLOCK + 8, 8), BLOCK)
        head, conduct = pk[0, 0, prow, :], pk[1, 0, prow, :]
        v_prev = flux_prev = q_prev = None
        for k in range(LAY):
            target = -lat[k, rows, :]
            diag = stor[k, rows, :] + gsum[k, rows, :]
            if k < LAY - 1:
                head_n, conduct_n = pk[0, k + 1, prow, :], pk[1, k + 1, prow, :]
                v = 2.0 * (conduct + conduct_n)
                flux = v * (head - head_n + 1.0)
                diag = diag + v
                target = target - flux
            else:
                target = target - 4.0 * conduct
            if k > 0:
                target = target + flux_prev
                diag = diag + v_prev - v_prev * q_prev
            inv = 1.0 / diag
            rinv[k, rows, :] = inv
            rhs[k, rows, :] = target * inv
            if k > 0:
                low[k, rows, :] = v_prev * inv
            if k < LAY - 1:
                q_prev = v * inv
                upp[k, rows, :] = q_prev
                head, conduct, v_prev, flux_prev = head_n, conduct_n, v, flux
        return carry

    lax.fori_loop(0, RX // BLOCK, factor_first, 0)

    iota_c = lax.broadcasted_iota(I32, (256, 128), 0)
    iota_r = lax.broadcasted_iota(I32, (32, 128), 0)
    acc[...] = jnp.zeros_like(acc)

    def place(g, carry):
        sx = lax.rem(bx + g, NX)
        pltpu.make_async_copy(recv.at[sx], recv.at[sx], recv_sem.at[sx]).wait()
        for j in range(NY // 2):
            m0, m1 = recv[sx, 2 * j], recv[sx, 2 * j + 1]
            v0 = jnp.where(first_half, m0, pltpu.roll(m1, 64, 1))
            v1 = jnp.where(first_half, pltpu.roll(m0, 64, 1), m1)
            at = slice(j * 128, (j + 1) * 128)
            spot = v1[7:8, :].astype(I32)
            brow = spot >> 7
            col = (spot & 127) + ((brow >> 5) << 7)
            brow = brow & 31
            row_of[sx, :, at] = brow
            b_mat[sx, :, at] = jnp.where(iota_c == col, 1.0, 0.0).astype(BF16)
            hit = iota_r == brow
            h0 = v0.astype(BF16).astype(F32)
            h1 = v1.astype(BF16).astype(F32)
            l0, l1 = v0 - h0, v1 - h1
            for f in range(FIELDS):
                hi = h0[f : f + 1] if f < 8 else h1[f - 8 : f - 7]
                lo = l0[f : f + 1] if f < 8 else l1[f - 8 : f - 7]
                a_mat[f * 64 : f * 64 + 32, at] = jnp.where(hit, hi, 0.0).astype(BF16)
                a_mat[f * 64 + 32 : f * 64 + 64, at] = jnp.where(hit, lo, 0.0).astype(BF16)
        acc[...] += lax.dot_general(
            a_mat[...], b_mat[sx], (((1,), (1,)), ((), ())), preferred_element_type=F32
        )
        return carry

    lax.fori_loop(0, NX, place, 0)
    for f in range(FIELDS):
        both = acc[f * 64 : f * 64 + 32, :] + acc[f * 64 + 32 : f * 64 + 64, :]
        grid[f, 0:32, :] = both[:, :128]
        grid[f, 32:64, :] = both[:, 128:]
    lane_b = lax.broadcasted_iota(I32, (BLOCK, 128), 1)
    pair_b = lane_b // 2

    def solve_first(r, carry):
        rows = pl.ds(pl.multiple_of(r * BLOCK, BLOCK), BLOCK)
        prow = pl.ds(pl.multiple_of(r * BLOCK + 8, 8), BLOCK)
        last = rhs[0, rows, :] + (grid[ROOT, rows, :] - grid[0, rows, :]) * rinv[0, rows, :]
        val[0, rows, :] = last
        for k in range(1, LAY):
            here = rhs[k, rows, :]
            if k < ROOT:
                here = here - grid[k, rows, :] * rinv[k, rows, :]
            last = here + low[k, rows, :] * last
            val[k, rows, :] = last
        packed = jnp.zeros((BLOCK, 128), F32)
        for k in range(LAY - 1, -1, -1):
            if k < LAY - 1:
                last = val[k, rows, :] + upp[k, rows, :] * last
            head = pk[0, k, prow, :] + last
            width = par_w[k, rows, :]
            sq, conduct, storage = closures(
                head, par_a[k, rows, :], par_n[k, rows, :], par_e[k, rows, :],
                par_k[k, rows, :], width,
            )
            pk[0, k, prow, :] = head
            pk[1, k, prow, :] = conduct
            stor[k, rows, :] = storage
            rhs[k, rows, :] = 2.0 * width * (sat_old[k, rows, :] - sq * sq)
            packed = jnp.where(pair_b == k, pltpu.roll(head, 2 * k + 1, 1), packed)
            packed = jnp.where(pair_b == k + 32, pltpu.roll(conduct, 2 * k + 65, 1), packed)
        ypack[1, rows, :] = packed
        return carry

    lax.fori_loop(0, RX // BLOCK, solve_first, 0)

    moves = halo_copies(1)
    for move in moves:
        move.start()
    halo_finish(1, moves)
    lax.fori_loop(0, LAY, sideways, 0)

    def solve_second(r, carry):
        rows = pl.ds(pl.multiple_of(r * BLOCK, BLOCK), BLOCK)
        prow = pl.ds(pl.multiple_of(r * BLOCK + 8, 8), BLOCK)
        head, conduct = pk[0, 0, prow, :], pk[1, 0, prow, :]
        v_prev = flux_prev = q_prev = last = None
        for k in range(LAY):
            target = rhs[k, rows, :] - lat[k, rows, :]
            if k < ROOT:
                target = target - grid[k, rows, :]
            diag = stor[k, rows, :] + gsum[k, rows, :]
            if k < LAY - 1:
                head_n, conduct_n = pk[0, k + 1, prow, :], pk[1, k + 1, prow, :]
                v = 2.0 * (conduct + conduct_n)
                flux = v * (head - head_n + 1.0)
                diag = diag + v
                target = target - flux
            else:
                target = target - 4.0 * conduct
            if k > 0:
                target = target + flux_prev + v_prev * last
                diag = diag + v_prev - v_prev * q_prev
            else:
                target = target + grid[ROOT, rows, :]
            inv = 1.0 / diag
            last = target * inv
            val[k, rows, :] = last
            if k < LAY - 1:
                q_prev = v * inv
                upp[k, rows, :] = q_prev
                head, conduct, v_prev, flux_prev = head_n, conduct_n, v, flux
        numer = denom = jnp.zeros((BLOCK, 128), F32)
        for k in range(LAY - 1, -1, -1):
            if k < LAY - 1:
                last = val[k, rows, :] + upp[k, rows, :] * last
            head = pk[0, k, prow, :] + last
            val[k, rows, :] = head
            if k < ROOT:
                log_s = par_n[k, rows, :] * jnp.log2(
                    par_a[k, rows, :] * jnp.maximum(-head, TINY)
                )
                sat = jnp.exp2(-par_e[k, rows, :] * jnp.log2(1.0 + jnp.exp2(log_s)))
                weight = grid[k, rows, :]
                numer = numer + weight * sat
                denom = denom + weight
        gsum[0, rows, :] = numer / jnp.maximum(denom, TINY)
        return carry

    lax.fori_loop(0, RX // BLOCK, solve_second, 0)
    out_copy = pltpu.make_async_copy(val, p_out, out_sem)
    out_copy.start()

    state = jnp.concatenate([gsum[0, 0:32, :], gsum[0, 32:64, :]], axis=1)
    s_hi = state.astype(BF16)
    left = state - s_hi.astype(F32)
    s_mid = left.astype(BF16)
    s_low = (left - s_mid.astype(F32)).astype(BF16)
    pieces = jnp.concatenate([s_hi, s_mid, s_low], axis=0)
    iota_r1 = lax.broadcasted_iota(I32, (32, 1024), 0)

    def fetch(g, carry):
        got = lax.dot_general(
            pieces, b_mat[g], (((1,), (0,)), ((), ())), preferred_element_type=F32
        )
        got = got[0:32] + got[32:64] + got[64:96]
        line = jnp.sum(jnp.where(iota_r1 == row_of[g], got, 0.0), axis=0, keepdims=True)
        for j in range(8):
            back[g * 8 + j] = line[:, j * 128 : (j + 1) * 128]
        return carry

    lax.fori_loop(0, NX, fetch, 0)

    own_back = pltpu.make_async_copy(back.at[me // 2], mine.at[me], ret_recv)
    own_back.start()

    def reply(i, carry):
        tx, ty = peer(i)
        pltpu.make_async_remote_copy(
            back.at[(tx * NY + ty) // 2], mine.at[me], ret_send, ret_recv,
            device_id=(tx, ty), device_id_type=MESH,
        ).start()
        return carry

    lax.fori_loop(1, PEERS, reply, 0)
    pltpu.make_async_copy(mine, mine, ret_recv).wait()

    parity = lax.rem(me, 2)
    lane1 = lax.broadcasted_iota(I32, (1, 128), 1)

    def take(q, carry):
        even, other = mine[2 * q], mine[2 * q + 1]
        low_half = jnp.where(lane1 < 64, even, pltpu.roll(other, 64, 1))
        high_half = jnp.where(lane1 < 64, pltpu.roll(even, 64, 1), other)
        s_out[q] = jnp.where(parity == 0, low_half, high_half)
        return carry

    lax.fori_loop(0, PEERS // 2, take, 0)

    pltpu.make_async_copy(send.at[0 : PEERS - 1], send.at[0 : PEERS - 1], send_sem).wait()
    pltpu.make_async_copy(mine.at[0 : PEERS - 1], mine.at[0 : PEERS - 1], ret_send).wait()
    out_copy.wait()


def on_device(h_old, soil_type, ks_scale, soil_table, clump_brick, clump_cell, root_fraction,
              transpiration, infiltration):
    del clump_brick
    whole = lambda shape, dtype=F32: pltpu.VMEM(shape, dtype)
    cube = whole((LAY, RX, RY))
    dma = pltpu.SemaphoreType.DMA
    vmem = pl.BlockSpec(memory_space=pltpu.VMEM)
    hbm = pl.BlockSpec(memory_space=pl.ANY)
    scratch = [
        cube, whole((LAY, RX, RY), I32), cube,
        whole((1, SLOTS), I32), whole((ROOT, SLOTS)), whole((1, SLOTS)), whole((1, SLOTS)),
        whole((8, 128)), whole((8, SLOTS)), whole((PEERS, 8, 128)), whole((NX, NY, 8, 128)),
        cube, cube, cube, cube, cube,
        whole((2, LAY, RX + 16, RY)), cube, cube, cube, cube,
        cube, cube, cube, cube, cube,
        whole((FIELDS * 64, 1024), BF16), whole((NX, 256, 1024), BF16),
        whole((NX, 1, 1024), I32), whole((FIELDS * 64, 256)), whole((FIELDS, RX, RY)),
        whole((2, RX, 128)), whole((2, 2, RX, 128)), whole((2, 2, 2, LAY, 8, 128)),
        whole((RX, 128)),
        whole((PEERS // 2, 1, 128)), whole((PEERS, 1, 128)),
        dma((7,)), dma, dma((NX,)), dma((2, 4)), dma((2, 4)), dma, dma, dma,
    ]
    pressure, stress = pl.pallas_call(
        kernel,
        out_shape=(
            jax.ShapeDtypeStruct((LAY, RX, RY), F32),
            jax.ShapeDtypeStruct((PEERS // 2, 1, 128), F32),
        ),
        in_specs=[hbm, hbm, hbm, vmem, hbm, hbm, hbm, hbm],
        out_specs=(hbm, vmem),
        scratch_shapes=scratch,
        compiler_params=pltpu.CompilerParams(
            collective_id=1, has_side_effects=True, vmem_limit_bytes=56 * 1024 * 1024
        ),
        name="step",
    )(
        h_old, soil_type, ks_scale, soil_table, clump_cell.reshape(1, SLOTS), root_fraction,
        transpiration.reshape(1, SLOTS), infiltration.reshape(1, SLOTS),
    )
    return pressure, stress.reshape(SLOTS)


def solution(mesh):
    cells = P(None, "bx", "by")
    slots = P(("bx", "by"))
    return jax.shard_map(
        on_device,
        mesh=mesh,
        in_specs=(cells, cells, cells, P(), slots, slots, P(None, ("bx", "by")), slots, slots),
        out_specs=(cells, slots),
        check_vma=False,
    )
```

```python
import itertools

import jax
import jax.numpy as jnp
from jax import lax
from jax.experimental import pallas as pl
from jax.experimental.pallas import tpu as pltpu
from jax.sharding import PartitionSpec as P

MESH = pl.DeviceIdType.MESH
NX, NY = 8, 16
PEERS = NX * NY
LAY, ROOT = 20, 14
RX, RY = 64, 128
SLOTS = RX * RY
FIELDS = ROOT + 1
BLOCK = 16
TINY = 1e-30
F32, BF16, I32 = jnp.float32, jnp.bfloat16, jnp.int32


ORDER = sorted(
    (o for o in itertools.product(range(4), range(2), range(4), range(4)) if any(o)),
    key=lambda o: -sum(min(d, 4 - d) for d in (o[0], o[2], o[3])),
)


def closures(head, alpha, shape_n, exponent, ks, width):
    log_s = shape_n * jnp.log2(alpha * jnp.maximum(-head, TINY))
    log_b = jnp.log2(1.0 + jnp.exp2(log_s))
    log_w = exponent * (log_s - log_b)
    root = jnp.exp2(-0.5 * exponent * log_b)
    inner = 1.0 - jnp.exp2(log_w)
    conduct = ks * root * (inner * inner)
    storage = 0.4 + 2.0 * width * (shape_n - 1.0) * alpha * jnp.exp2(log_w - log_b)
    return root, conduct, storage


def kernel(
    h_hbm, soil_hbm, ks_hbm, table_ref, cell_hbm, root_hbm, transp_hbm, infil_hbm,
    p_out, s_out,
    h, soil, ks_in, cell, root, transp, infil,
    table, fields1, send, recv,
    par_a, par_n, par_e, par_k, par_w,
    pk, sat_old, stor, lat, gsum,
    rinv, low, upp, rhs, val,
    a_mat, b_mat, row_of, acc, grid,
    ypack, yrecv, xrecv, ycomb, state_ref,
    back, mine,
    in_sem, send_sem, recv_sem, halo_send, halo_recv, ret_send, ret_recv, out_sem,
):
    bx = lax.axis_index("bx")
    by = lax.axis_index("by")
    me = bx * NY + by

    copies = [
        pltpu.make_async_copy(src, dst, in_sem.at[i])
        for i, (src, dst) in enumerate(
            (
                (root_hbm, root), (transp_hbm, transp), (infil_hbm, infil), (cell_hbm, cell),
                (h_hbm, h), (soil_hbm, soil), (ks_hbm, ks_in),
            )
        )
    ]
    for copy in copies:
        copy.start()

    core = lax.rem(bx, 2)
    cores = (core, 1 - core)
    ys = [lax.rem(bx // 2 + d, 4) * 2 for d in range(4)]
    xs = [lax.rem(by // 4 + d, 4) * 4 for d in range(4)]
    zs = [lax.rem(by + d, 4) for d in range(4)]

    def peer(offset):
        y, c, x, z = offset
        return ys[y] + cores[c], xs[x] + zs[z]

    barrier = pltpu.get_barrier_semaphore()
    for offset in ORDER:
        pl.semaphore_signal(barrier, inc=1, device_id=peer(offset), device_id_type=MESH)

    lane8 = lax.broadcasted_iota(I32, (8, 128), 1)
    sub8 = lax.broadcasted_iota(I32, (8, 128), 0)
    first_half = lane8 < 64

    for copy in copies[:4]:
        copy.wait()
    fields1[0:6, :] = root[8:14, :]
    fields1[6:7, :] = infil[...]
    fields1[7:8, :] = cell[...].astype(F32)

    def pack(q, carry):
        at = pl.ds(pl.multiple_of(q * 128, 128), 128)
        demand = transp[:, at]
        v0 = root[0:8, at] * demand
        v1 = fields1[:, at] * jnp.where(sub8 < 6, demand, 1.0)
        r0 = pltpu.roll(v0, 64, 1)
        r1 = pltpu.roll(v1, 64, 1)
        send[2 * q] = jnp.where(first_half, v0, r1)
        send[2 * q + 1] = jnp.where(first_half, r0, v1)
        return carry

    lax.fori_loop(0, PEERS // 2, pack, 0, unroll=8)

    pl.semaphore_wait(barrier, PEERS - 1)

    own = pltpu.make_async_copy(send.at[me], recv.at[bx, by], recv_sem.at[bx])
    own.start()

    for offset in ORDER:
        tx, ty = peer(offset)
        pltpu.make_async_remote_copy(
            send.at[tx * NY + ty], recv.at[bx, by], send_sem, recv_sem.at[bx],
            device_id=(tx, ty), device_id_type=MESH,
        ).start()

    table[...] = jnp.zeros_like(table)
    table[0:4, 0:12] = table_ref[...]
    for copy in copies[4:]:
        copy.wait()
    t0, t1, t2, t3 = (jnp.broadcast_to(table[i : i + 1, :], (RX, 128)) for i in range(4))
    lane = lax.broadcasted_iota(I32, (RX, 128), 1)

    def first(k, packed):
        kind = soil[k]
        look = lambda t: jnp.take_along_axis(t, kind, axis=1, mode="promise_in_bounds")
        alpha = 4.0 * look(t0)
        shape_n = 1.2 + 2.0 * look(t1)
        ks = 0.75 * look(t2) * ks_in[k]
        width = 0.25 + 0.3 * look(t3)
        exponent = 1.0 - 1.0 / shape_n
        par_a[k], par_n[k], par_e[k], par_k[k], par_w[k] = alpha, shape_n, exponent, ks, width
        head = h[k]
        sq, conduct, storage = closures(head, alpha, shape_n, exponent, ks, width)
        sat_old[k] = sq * sq
        stor[k] = storage
        pk[0, k, 8 : 8 + RX, :] = head
        pk[1, k, 8 : 8 + RX, :] = conduct
        turn = 2 * k + 1
        pair = lane // 2
        packed = jnp.where(pair == k, pltpu.roll(head, turn, 1), packed)
        packed = jnp.where(pair == k + 32, pltpu.roll(conduct, turn + 64, 1), packed)
        return packed

    ypack[0] = lax.fori_loop(0, LAY, first, jnp.zeros((RX, 128), F32))

    def halo_copies(step):
        up = lax.rem(bx + NX - 1, NX), by
        down = lax.rem(bx + 1, NX), by
        left = bx, lax.rem(by + NY - 1, NY)
        right = bx, lax.rem(by + 1, NY)
        moves = (
            (pk.at[:, :, pl.ds(71, 1), :], xrecv.at[step, 0, :, :, pl.ds(0, 1), :], down),
            (pk.at[:, :, pl.ds(8, 1), :], xrecv.at[step, 1, :, :, pl.ds(0, 1), :], up),
            (ypack.at[step], yrecv.at[step, 0], right),
            (ypack.at[step], yrecv.at[step, 1], left),
        )
        return [
            pltpu.make_async_remote_copy(
                src, dst, halo_send.at[step, i], halo_recv.at[step, i],
                device_id=to, device_id_type=MESH,
            )
            for i, (src, dst, to) in enumerate(moves)
        ]

    odd = lax.rem(lane, 2) == 1
    lane_b = lax.broadcasted_iota(I32, (BLOCK, 128), 1)
    pair_b = lane_b // 2

    def halo_finish(step, moves):
        for move in moves:
            move.wait_recv()
        for move in moves:
            move.wait_send()
        own = ypack[step]
        both = jnp.where(
            odd, pltpu.roll(yrecv[step, 0], 1, 1), pltpu.roll(yrecv[step, 1], 127, 1)
        )
        edge = jnp.logical_or(
            jnp.logical_and(odd, by == 0), jnp.logical_and(jnp.logical_not(odd), by == NY - 1)
        )
        both = jnp.where(edge, -own, both)
        face = pltpu.roll(own + both, 64, 1)
        flow = face * (own - both)
        ycomb[...] = jnp.where(lane < 64, flow, own + both)
        for k in range(LAY):
            for side, row, off in ((0, 0, bx == 0), (1, RX - 1, bx == NX - 1)):
                p_own, k_own = pk[0, k, 8 + row : 9 + row, :], pk[1, k, 8 + row : 9 + row, :]
                g = k_own + jnp.where(off, -k_own, xrecv[step, side, 1, k, 0:1, :])
                gsum[k, row : row + 1, :] += g
                lat[k, row : row + 1, :] += g * (p_own - xrecv[step, side, 0, k, 0:1, :])

    at_first = lane == 0

    def sideways(k, carry):
        head, conduct = pk[0, k, 8:72, :], pk[1, k, 8:72, :]
        g = jnp.where(at_first, 0.0, conduct + pltpu.roll(conduct, 1, 1))
        f = g * (head - pltpu.roll(head, 1, 1))
        gx = conduct[:-1] + conduct[1:]
        fx = gx * (head[1:] - head[:-1])
        zero = jnp.zeros((1, 128), F32)
        gx0 = jnp.concatenate([zero, gx], axis=0)
        gx1 = jnp.concatenate([gx, zero], axis=0)
        fx0 = jnp.concatenate([zero, fx], axis=0)
        fx1 = jnp.concatenate([fx, zero], axis=0)
        gsum[k] = (g + pltpu.roll(g, 127, 1)) + (gx0 + gx1)
        lat[k] = (f - pltpu.roll(f, 127, 1)) + (fx0 - fx1)
        return carry

    moves = halo_copies(0)
    for move in moves:
        move.start()
    lax.fori_loop(0, LAY, sideways, 0)
    halo_finish(0, moves)
    ends = jnp.logical_or(lane_b == 0, lane_b == 127)

    def factor_first(r, carry):
        rows = pl.ds(pl.multiple_of(r * BLOCK, BLOCK), BLOCK)
        prow = pl.ds(pl.multiple_of(r * BLOCK + 8, 8), BLOCK)
        head, conduct = pk[0, 0, prow, :], pk[1, 0, prow, :]
        v_prev = flux_prev = q_prev = None
        for k in range(LAY):
            comb = ycomb[rows, :]
            side_f = jnp.where(ends, pltpu.roll(comb, 127 - 2 * k, 1), 0.0)
            side_g = jnp.where(ends, pltpu.roll(comb, 63 - 2 * k, 1), 0.0)
            target = -(lat[k, rows, :] + side_f)
            diag = stor[k, rows, :] + (gsum[k, rows, :] + side_g)
            if k < LAY - 1:
                head_n, conduct_n = pk[0, k + 1, prow, :], pk[1, k + 1, prow, :]
                v = 2.0 * (conduct + conduct_n)
                flux = v * (head - head_n + 1.0)
                diag = diag + v
                target = target - flux
            else:
                target = target - 4.0 * conduct
            if k > 0:
                target = target + flux_prev
                diag = diag + v_prev - v_prev * q_prev
            inv = 1.0 / diag
            rinv[k, rows, :] = inv
            rhs[k, rows, :] = target * inv
            if k > 0:
                low[k, rows, :] = v_prev * inv
            if k < LAY - 1:
                q_prev = v * inv
                upp[k, rows, :] = q_prev
                head, conduct, v_prev, flux_prev = head_n, conduct_n, v, flux
        return carry

    lax.fori_loop(0, RX // BLOCK, factor_first, 0)

    iota_c = lax.broadcasted_iota(I32, (256, 128), 0)
    iota_r = lax.broadcasted_iota(I32, (32, 128), 0)
    acc[...] = jnp.zeros_like(acc)

    def place(g, carry):
        sx = lax.rem(bx + g, NX)
        pltpu.make_async_copy(recv.at[sx], recv.at[sx], recv_sem.at[sx]).wait()
        for j in range(NY // 2):
            m0, m1 = recv[sx, 2 * j], recv[sx, 2 * j + 1]
            v0 = jnp.where(first_half, m0, pltpu.roll(m1, 64, 1))
            v1 = jnp.where(first_half, pltpu.roll(m0, 64, 1), m1)
            at = slice(j * 128, (j + 1) * 128)
            spot = v1[7:8, :].astype(I32)
            brow = spot >> 7
            col = (spot & 127) + ((brow >> 5) << 7)
            brow = brow & 31
            row_of[sx, :, at] = brow
            b_mat[sx, :, at] = jnp.where(iota_c == col, 1.0, 0.0).astype(BF16)
            hit = iota_r == brow
            h0 = v0.astype(BF16).astype(F32)
            h1 = v1.astype(BF16).astype(F32)
            l0, l1 = v0 - h0, v1 - h1
            for f in range(FIELDS):
                hi = h0[f : f + 1] if f < 8 else h1[f - 8 : f - 7]
                lo = l0[f : f + 1] if f < 8 else l1[f - 8 : f - 7]
                a_mat[f * 64 : f * 64 + 32, at] = jnp.where(hit, hi, 0.0).astype(BF16)
                a_mat[f * 64 + 32 : f * 64 + 64, at] = jnp.where(hit, lo, 0.0).astype(BF16)
        acc[...] += lax.dot_general(
            a_mat[...], b_mat[sx], (((1,), (1,)), ((), ())), preferred_element_type=F32
        )
        return carry

    lax.fori_loop(0, NX, place, 0)
    for f in range(FIELDS):
        both = acc[f * 64 : f * 64 + 32, :] + acc[f * 64 + 32 : f * 64 + 64, :]
        grid[f, 0:32, :] = both[:, :128]
        grid[f, 32:64, :] = both[:, 128:]
    def solve_first(r, carry):
        rows = pl.ds(pl.multiple_of(r * BLOCK, BLOCK), BLOCK)
        prow = pl.ds(pl.multiple_of(r * BLOCK + 8, 8), BLOCK)
        last = rhs[0, rows, :] + (grid[ROOT, rows, :] - grid[0, rows, :]) * rinv[0, rows, :]
        val[0, rows, :] = last
        for k in range(1, LAY):
            here = rhs[k, rows, :]
            if k < ROOT:
                here = here - grid[k, rows, :] * rinv[k, rows, :]
            last = here + low[k, rows, :] * last
            val[k, rows, :] = last
        packed = jnp.zeros((BLOCK, 128), F32)
        for k in range(LAY - 1, -1, -1):
            if k < LAY - 1:
                last = val[k, rows, :] + upp[k, rows, :] * last
            head = pk[0, k, prow, :] + last
            width = par_w[k, rows, :]
            sq, conduct, storage = closures(
                head, par_a[k, rows, :], par_n[k, rows, :], par_e[k, rows, :],
                par_k[k, rows, :], width,
            )
            pk[0, k, prow, :] = head
            pk[1, k, prow, :] = conduct
            stor[k, rows, :] = storage
            rhs[k, rows, :] = 2.0 * width * (sat_old[k, rows, :] - sq * sq)
            packed = jnp.where(pair_b == k, pltpu.roll(head, 2 * k + 1, 1), packed)
            packed = jnp.where(pair_b == k + 32, pltpu.roll(conduct, 2 * k + 65, 1), packed)
        ypack[1, rows, :] = packed
        return carry

    lax.fori_loop(0, RX // BLOCK, solve_first, 0)

    moves = halo_copies(1)
    for move in moves:
        move.start()
    lax.fori_loop(0, LAY, sideways, 0)
    halo_finish(1, moves)

    def solve_second(r, carry):
        rows = pl.ds(pl.multiple_of(r * BLOCK, BLOCK), BLOCK)
        prow = pl.ds(pl.multiple_of(r * BLOCK + 8, 8), BLOCK)
        head, conduct = pk[0, 0, prow, :], pk[1, 0, prow, :]
        v_prev = flux_prev = q_prev = last = None
        for k in range(LAY):
            comb = ycomb[rows, :]
            side_f = jnp.where(ends, pltpu.roll(comb, 127 - 2 * k, 1), 0.0)
            side_g = jnp.where(ends, pltpu.roll(comb, 63 - 2 * k, 1), 0.0)
            target = rhs[k, rows, :] - (lat[k, rows, :] + side_f)
            if k < ROOT:
                target = target - grid[k, rows, :]
            diag = stor[k, rows, :] + (gsum[k, rows, :] + side_g)
            if k < LAY - 1:
                head_n, conduct_n = pk[0, k + 1, prow, :], pk[1, k + 1, prow, :]
                v = 2.0 * (conduct + conduct_n)
                flux = v * (head - head_n + 1.0)
                diag = diag + v
                target = target - flux
            else:
                target = target - 4.0 * conduct
            if k > 0:
                target = target + flux_prev + v_prev * last
                diag = diag + v_prev - v_prev * q_prev
            else:
                target = target + grid[ROOT, rows, :]
            inv = 1.0 / diag
            last = target * inv
            val[k, rows, :] = last
            if k < LAY - 1:
                q_prev = v * inv
                upp[k, rows, :] = q_prev
                head, conduct, v_prev, flux_prev = head_n, conduct_n, v, flux
        numer = denom = jnp.zeros((BLOCK, 128), F32)
        for k in range(LAY - 1, -1, -1):
            if k < LAY - 1:
                last = val[k, rows, :] + upp[k, rows, :] * last
            head = pk[0, k, prow, :] + last
            val[k, rows, :] = head
            if k < ROOT:
                log_s = par_n[k, rows, :] * jnp.log2(
                    par_a[k, rows, :] * jnp.maximum(-head, TINY)
                )
                sat = jnp.exp2(-par_e[k, rows, :] * jnp.log2(1.0 + jnp.exp2(log_s)))
                weight = grid[k, rows, :]
                numer = numer + weight * sat
                denom = denom + weight
        state_ref[rows, :] = numer / jnp.maximum(denom, TINY)
        return carry

    lax.fori_loop(0, RX // BLOCK, solve_second, 0)
    out_copy = pltpu.make_async_copy(val, p_out, out_sem)
    out_copy.start()

    state = jnp.concatenate([state_ref[0:32, :], state_ref[32:64, :]], axis=1)
    s_hi = state.astype(BF16)
    left = state - s_hi.astype(F32)
    s_mid = left.astype(BF16)
    s_low = (left - s_mid.astype(F32)).astype(BF16)
    pieces = jnp.concatenate([s_hi, s_mid, s_low], axis=0)
    iota_r1 = lax.broadcasted_iota(I32, (32, 1024), 0)

    def fetch(g, carry):
        got = lax.dot_general(
            pieces, b_mat[g], (((1,), (0,)), ((), ())), preferred_element_type=F32
        )
        got = got[0:32] + got[32:64] + got[64:96]
        line = jnp.sum(jnp.where(iota_r1 == row_of[g], got, 0.0), axis=0, keepdims=True)
        for j in range(8):
            back[g * 8 + j] = line[:, j * 128 : (j + 1) * 128]
        return carry

    lax.fori_loop(0, NX, fetch, 0)

    own_back = pltpu.make_async_copy(back.at[me // 2], mine.at[me], ret_recv)
    own_back.start()

    for offset in ORDER:
        tx, ty = peer(offset)
        pltpu.make_async_remote_copy(
            back.at[(tx * NY + ty) // 2], mine.at[me], ret_send, ret_recv,
            device_id=(tx, ty), device_id_type=MESH,
        ).start()
    pltpu.make_async_copy(mine, mine, ret_recv).wait()

    even, other = mine[pl.ds(0, 64, 2), 0, :], mine[pl.ds(1, 64, 2), 0, :]
    low_half = jnp.where(lane < 64, even, pltpu.roll(other, 64, 1))
    high_half = jnp.where(lane < 64, pltpu.roll(even, 64, 1), other)
    s_out[...] = jnp.where(lax.rem(me, 2) == 0, low_half, high_half)

    pltpu.make_async_copy(send.at[0 : PEERS - 1], send.at[0 : PEERS - 1], send_sem).wait()
    pltpu.make_async_copy(mine.at[0 : PEERS - 1], mine.at[0 : PEERS - 1], ret_send).wait()
    out_copy.wait()


def on_device(h_old, soil_type, ks_scale, soil_table, clump_brick, clump_cell, root_fraction,
              transpiration, infiltration):
    del clump_brick
    whole = lambda shape, dtype=F32: pltpu.VMEM(shape, dtype)
    cube = whole((LAY, RX, RY))
    dma = pltpu.SemaphoreType.DMA
    vmem = pl.BlockSpec(memory_space=pltpu.VMEM)
    hbm = pl.BlockSpec(memory_space=pl.ANY)
    scratch = [
        cube, whole((LAY, RX, RY), I32), cube,
        whole((1, SLOTS), I32), whole((ROOT, SLOTS)), whole((1, SLOTS)), whole((1, SLOTS)),
        whole((8, 128)), whole((8, SLOTS)), whole((PEERS, 8, 128)), whole((NX, NY, 8, 128)),
        cube, cube, cube, cube, cube,
        whole((2, LAY, RX + 16, RY)), cube, cube, cube, cube,
        cube, cube, cube, cube, cube,
        whole((FIELDS * 64, 1024), BF16), whole((NX, 256, 1024), BF16),
        whole((NX, 1, 1024), I32), whole((FIELDS * 64, 256)), whole((FIELDS, RX, RY)),
        whole((2, RX, 128)), whole((2, 2, RX, 128)), whole((2, 2, 2, LAY, 8, 128)),
        whole((RX, 128)), whole((RX, 128)),
        whole((PEERS // 2, 1, 128)), whole((PEERS, 1, 128)),
        dma((7,)), dma, dma((NX,)), dma((2, 4)), dma((2, 4)), dma, dma, dma,
    ]
    pressure, stress = pl.pallas_call(
        kernel,
        out_shape=(
            jax.ShapeDtypeStruct((LAY, RX, RY), F32),
            jax.ShapeDtypeStruct((PEERS // 2, 128), F32),
        ),
        in_specs=[hbm, hbm, hbm, vmem, hbm, hbm, hbm, hbm],
        out_specs=(hbm, vmem),
        scratch_shapes=scratch,
        compiler_params=pltpu.CompilerParams(
            collective_id=1, has_side_effects=True, vmem_limit_bytes=56 * 1024 * 1024
        ),
        name="step",
    )(
        h_old, soil_type, ks_scale, soil_table, clump_cell.reshape(1, SLOTS), root_fraction,
        transpiration.reshape(1, SLOTS), infiltration.reshape(1, SLOTS),
    )
    return pressure, stress.reshape(SLOTS)


def solution(mesh):
    cells = P(None, "bx", "by")
    slots = P(("bx", "by"))
    return jax.shard_map(
        on_device,
        mesh=mesh,
        in_specs=(cells, cells, cells, P(), slots, slots, P(None, ("bx", "by")), slots, slots),
        out_specs=(cells, slots),
        check_vma=False,
    )
```

```python
import itertools

import jax
import jax.numpy as jnp
from jax import lax
from jax.experimental import pallas as pl
from jax.experimental.pallas import tpu as pltpu
from jax.sharding import PartitionSpec as P

MESH = pl.DeviceIdType.MESH
NX, NY = 8, 16
PEERS = NX * NY
LAY, ROOT = 20, 14
RX, RY = 64, 128
SLOTS = RX * RY
FIELDS = ROOT + 1
BLOCK = 16
TINY = 1e-30
F32, BF16, I32 = jnp.float32, jnp.bfloat16, jnp.int32


def ring(d):
    return min(d, 4 - d)


PAIRS = sorted(
    itertools.product(range(4), range(2), range(4), range(2)),
    key=lambda o: (ring(o[0]) + ring(o[2]) + o[3], o[1], ring(o[0])),
)
GROUPS, PER = 8, 8
WAVES = (0, 1, 2, 3, 4, 5, 6, 7)
PLACE = {
    pair: wave * PER + i
    for wave, group in enumerate(WAVES)
    for i, pair in enumerate(PAIRS[group * PER : group * PER + PER])
}
OWN = PLACE[0, 0, 0, 0]
TARGETS = [
    (pair, b)
    for group in WAVES
    for pair in reversed(PAIRS[group * PER : group * PER + PER])
    for b in (1, 0)
    if any(pair) or b
]


def seen_back(pair):
    return PLACE[-pair[0] % 4, pair[1], -pair[2] % 4, pair[3]]


def closures(head, alpha, shape_n, exponent, ks, width):
    log_s = shape_n * jnp.log2(alpha * jnp.maximum(-head, TINY))
    log_b = jnp.log2(1.0 + jnp.exp2(log_s))
    log_w = exponent * (log_s - log_b)
    root = jnp.exp2(-0.5 * exponent * log_b)
    inner = 1.0 - jnp.exp2(log_w)
    conduct = ks * root * (inner * inner)
    storage = 0.4 + 2.0 * width * (shape_n - 1.0) * alpha * jnp.exp2(log_w - log_b)
    return root, conduct, storage


def kernel(
    h_hbm, soil_hbm, ks_hbm, table_ref, cell_hbm, root_hbm, transp_hbm, infil_hbm,
    p_out, s_out,
    h, soil, ks_in, cell, root, transp, infil,
    table, fields1, send, recv,
    par_a, par_n, par_e, par_k, par_w,
    pk, sat_old, stor, lat, gsum,
    rinv, low, upp, rhs, val,
    b_mat, row_of, acc, grid,
    ypack, yrecv, xrecv, ycomb, state_ref,
    back, mine,
    in_sem, send_sem, recv_sem, halo_send, halo_recv, ret_send, ret_recv, out_sem,
):
    bx = lax.axis_index("bx")
    by = lax.axis_index("by")
    me = bx * NY + by

    copies = [
        pltpu.make_async_copy(src, dst, in_sem.at[i])
        for i, (src, dst) in enumerate(
            (
                (root_hbm, root), (transp_hbm, transp), (infil_hbm, infil), (cell_hbm, cell),
                (h_hbm, h), (soil_hbm, soil), (ks_hbm, ks_in),
            )
        )
    ]
    for copy in copies:
        copy.start()

    core = lax.rem(bx, 2)
    cores = (core, 1 - core)
    ys = [lax.rem(bx // 2 + d, 4) * 2 for d in range(4)]
    xs = [lax.rem(by // 4 + d, 4) * 4 for d in range(4)]
    half = lax.rem(by, 2)
    halves = (half, 1 - half)
    upper = lax.rem(by, 4) - half
    zs = (upper, 2 - upper)

    def peer(target):
        (y, c, x, z), b = target
        return ys[y] + cores[c], xs[x] + zs[z] + halves[b]

    barrier = pltpu.get_barrier_semaphore()
    for target in TARGETS:
        pl.semaphore_signal(barrier, inc=1, device_id=peer(target), device_id_type=MESH)

    lane8 = lax.broadcasted_iota(I32, (8, 128), 1)
    sub8 = lax.broadcasted_iota(I32, (8, 128), 0)
    first_half = lane8 < 64

    for copy in copies[:4]:
        copy.wait()
    fields1[0:6, :] = root[8:14, :]
    fields1[6:7, :] = infil[...]
    fields1[7:8, :] = cell[...].astype(F32)

    def pack(q, carry):
        at = pl.ds(pl.multiple_of(q * 128, 128), 128)
        demand = transp[:, at]
        v0 = root[0:8, at] * demand
        v1 = fields1[:, at] * jnp.where(sub8 < 6, demand, 1.0)
        r0 = pltpu.roll(v0, 64, 1)
        r1 = pltpu.roll(v1, 64, 1)
        send[2 * q] = jnp.where(first_half, v0, r1)
        send[2 * q + 1] = jnp.where(first_half, r0, v1)
        return carry

    lax.fori_loop(0, PEERS // 2, pack, 0, unroll=8)

    table[...] = jnp.zeros_like(table)
    table[0:4, 0:12] = table_ref[...]
    for copy in copies[4:]:
        copy.wait()
    t0, t1, t2, t3 = (jnp.broadcast_to(table[i : i + 1, :], (RX, 128)) for i in range(4))
    lane = lax.broadcasted_iota(I32, (RX, 128), 1)

    def first(k, packed):
        kind = soil[k]
        look = lambda t: jnp.take_along_axis(t, kind, axis=1, mode="promise_in_bounds")
        alpha = 4.0 * look(t0)
        shape_n = 1.2 + 2.0 * look(t1)
        ks = 0.75 * look(t2) * ks_in[k]
        width = 0.25 + 0.3 * look(t3)
        exponent = 1.0 - 1.0 / shape_n
        par_a[k], par_n[k], par_e[k], par_k[k], par_w[k] = alpha, shape_n, exponent, ks, width
        head = h[k]
        sq, conduct, storage = closures(head, alpha, shape_n, exponent, ks, width)
        sat_old[k] = sq * sq
        stor[k] = storage
        pk[0, k, 8 : 8 + RX, :] = head
        pk[1, k, 8 : 8 + RX, :] = conduct
        turn = 2 * k + 1
        pair = lane // 2
        packed = jnp.where(pair == k, pltpu.roll(head, turn, 1), packed)
        packed = jnp.where(pair == k + 32, pltpu.roll(conduct, turn + 64, 1), packed)
        return packed

    ypack[0] = lax.fori_loop(0, LAY, first, jnp.zeros((RX, 128), F32))

    pl.semaphore_wait(barrier, PEERS - 1)

    def halo_copies(step):
        up = lax.rem(bx + NX - 1, NX), by
        down = lax.rem(bx + 1, NX), by
        left = bx, lax.rem(by + NY - 1, NY)
        right = bx, lax.rem(by + 1, NY)
        moves = (
            (pk.at[:, :, pl.ds(71, 1), :], xrecv.at[step, 0, :, :, pl.ds(0, 1), :], down),
            (pk.at[:, :, pl.ds(8, 1), :], xrecv.at[step, 1, :, :, pl.ds(0, 1), :], up),
            (ypack.at[step], yrecv.at[step, 0], right),
            (ypack.at[step], yrecv.at[step, 1], left),
        )
        return [
            pltpu.make_async_remote_copy(
                src, dst, halo_send.at[step, i], halo_recv.at[step, i],
                device_id=to, device_id_type=MESH,
            )
            for i, (src, dst, to) in enumerate(moves)
        ]

    odd = lax.rem(lane, 2) == 1
    lane_b = lax.broadcasted_iota(I32, (BLOCK, 128), 1)
    pair_b = lane_b // 2

    def halo_finish(step, moves):
        for move in moves:
            move.wait_recv()
        for move in moves:
            move.wait_send()
        own = ypack[step]
        both = jnp.where(
            odd, pltpu.roll(yrecv[step, 0], 1, 1), pltpu.roll(yrecv[step, 1], 127, 1)
        )
        edge = jnp.logical_or(
            jnp.logical_and(odd, by == 0), jnp.logical_and(jnp.logical_not(odd), by == NY - 1)
        )
        both = jnp.where(edge, -own, both)
        face = pltpu.roll(own + both, 64, 1)
        flow = face * (own - both)
        ycomb[...] = jnp.where(lane < 64, flow, own + both)
        for k in range(LAY):
            for side, row, off in ((0, 0, bx == 0), (1, RX - 1, bx == NX - 1)):
                p_own, k_own = pk[0, k, 8 + row : 9 + row, :], pk[1, k, 8 + row : 9 + row, :]
                g = k_own + jnp.where(off, -k_own, xrecv[step, side, 1, k, 0:1, :])
                gsum[k, row : row + 1, :] += g
                lat[k, row : row + 1, :] += g * (p_own - xrecv[step, side, 0, k, 0:1, :])

    at_first = lane == 0

    def sideways(k, carry):
        head, conduct = pk[0, k, 8:72, :], pk[1, k, 8:72, :]
        g = jnp.where(at_first, 0.0, conduct + pltpu.roll(conduct, 1, 1))
        f = g * (head - pltpu.roll(head, 1, 1))
        gx = conduct[:-1] + conduct[1:]
        fx = gx * (head[1:] - head[:-1])
        zero = jnp.zeros((1, 128), F32)
        gx0 = jnp.concatenate([zero, gx], axis=0)
        gx1 = jnp.concatenate([gx, zero], axis=0)
        fx0 = jnp.concatenate([zero, fx], axis=0)
        fx1 = jnp.concatenate([fx, zero], axis=0)
        gsum[k] = (g + pltpu.roll(g, 127, 1)) + (gx0 + gx1)
        lat[k] = (f - pltpu.roll(f, 127, 1)) + (fx0 - fx1)
        return carry

    moves = halo_copies(0)
    for move in moves:
        move.start()

    pltpu.make_async_copy(send.at[me], recv.at[OWN, half], recv_sem.at[OWN // PER]).start()
    for target in TARGETS:
        tx, ty = peer(target)
        spot = seen_back(target[0])
        pltpu.make_async_remote_copy(
            send.at[tx * NY + ty], recv.at[spot, half], send_sem, recv_sem.at[spot // PER],
            device_id=(tx, ty), device_id_type=MESH,
        ).start()

    lax.fori_loop(0, LAY, sideways, 0)
    iota_c = lax.broadcasted_iota(I32, (256, 128), 0)
    iota_r = lax.broadcasted_iota(I32, (32, 128), 0)
    acc[...] = jnp.zeros_like(acc)

    def spread_tile(g, j):
        m0, m1 = recv[g * PER + j, 0], recv[g * PER + j, 1]
        v0 = jnp.where(first_half, m0, pltpu.roll(m1, 64, 1))
        v1 = jnp.where(first_half, pltpu.roll(m0, 64, 1), m1)
        at = slice(j * 128, (j + 1) * 128)
        spot = v1[7:8, :].astype(I32)
        brow = spot >> 7
        col = (spot & 127) + ((brow >> 5) << 7)
        brow = brow & 31
        row_of[g, :, at] = brow
        b_mat[g, :, at] = jnp.where(iota_c == col, 1.0, 0.0).astype(BF16)
        hit = iota_r == brow
        spread = lambda line: jnp.where(hit, line, 0.0).astype(BF16)
        h0 = v0.astype(BF16).astype(F32)
        h1 = v1.astype(BF16).astype(F32)
        pieces = []
        for f in range(FIELDS):
            high, whole = (h0, v0) if f < 8 else (h1, v1)
            row = slice(f % 8, f % 8 + 1)
            pieces.append(spread(high[row]))
            pieces.append(spread((whole - high)[row]))
        return jnp.concatenate(pieces, axis=0)

    def place(g, carry):
        part_of = recv.at[pl.ds(g * PER, PER)]
        pltpu.make_async_copy(part_of, part_of, recv_sem.at[g]).wait()
        for part in range(PER // 2):
            blocks = []
            for j in range(part * 2, part * 2 + 2):
                blocks.append(spread_tile(g, j))
            a_val = jnp.concatenate(blocks, axis=1) if len(blocks) > 1 else blocks[0]
            acc[...] += lax.dot_general(
                a_val, b_mat[g, :, part * 256 : part * 256 + 256], (((1,), (1,)), ((), ())),
                preferred_element_type=F32,
            )
        return carry

    halo_finish(0, moves)
    ends = jnp.logical_or(lane_b == 0, lane_b == 127)

    def factor_first(r, carry):
        rows = pl.ds(pl.multiple_of(r * BLOCK, BLOCK), BLOCK)
        prow = pl.ds(pl.multiple_of(r * BLOCK + 8, 8), BLOCK)
        head, conduct = pk[0, 0, prow, :], pk[1, 0, prow, :]
        v_prev = flux_prev = q_prev = None
        for k in range(LAY):
            comb = ycomb[rows, :]
            side_f = jnp.where(ends, pltpu.roll(comb, 127 - 2 * k, 1), 0.0)
            side_g = jnp.where(ends, pltpu.roll(comb, 63 - 2 * k, 1), 0.0)
            target = -(lat[k, rows, :] + side_f)
            diag = stor[k, rows, :] + (gsum[k, rows, :] + side_g)
            if k < LAY - 1:
                head_n, conduct_n = pk[0, k + 1, prow, :], pk[1, k + 1, prow, :]
                v = 2.0 * (conduct + conduct_n)
                flux = v * (head - head_n + 1.0)
                diag = diag + v
                target = target - flux
            else:
                target = target - 4.0 * conduct
            if k > 0:
                target = target + flux_prev
                diag = diag + v_prev - v_prev * q_prev
            inv = 1.0 / diag
            rinv[k, rows, :] = inv
            rhs[k, rows, :] = target * inv
            if k > 0:
                low[k, rows, :] = v_prev * inv
            if k < LAY - 1:
                q_prev = v * inv
                upp[k, rows, :] = q_prev
                head, conduct, v_prev, flux_prev = head_n, conduct_n, v, flux
        return carry

    lax.fori_loop(0, RX // BLOCK, factor_first, 0)
    lax.fori_loop(0, GROUPS, place, 0)

    for f in range(FIELDS):
        both = acc[f * 64 : f * 64 + 32, :] + acc[f * 64 + 32 : f * 64 + 64, :]
        grid[f, 0:32, :] = both[:, :128]
        grid[f, 32:64, :] = both[:, 128:]
    def solve_first(r, carry):
        rows = pl.ds(pl.multiple_of(r * BLOCK, BLOCK), BLOCK)
        prow = pl.ds(pl.multiple_of(r * BLOCK + 8, 8), BLOCK)
        last = rhs[0, rows, :] + (grid[ROOT, rows, :] - grid[0, rows, :]) * rinv[0, rows, :]
        val[0, rows, :] = last
        for k in range(1, LAY):
            here = rhs[k, rows, :]
            if k < ROOT:
                here = here - grid[k, rows, :] * rinv[k, rows, :]
            last = here + low[k, rows, :] * last
            val[k, rows, :] = last
        packed = jnp.zeros((BLOCK, 128), F32)
        for k in range(LAY - 1, -1, -1):
            if k < LAY - 1:
                last = val[k, rows, :] + upp[k, rows, :] * last
            head = pk[0, k, prow, :] + last
            width = par_w[k, rows, :]
            sq, conduct, storage = closures(
                head, par_a[k, rows, :], par_n[k, rows, :], par_e[k, rows, :],
                par_k[k, rows, :], width,
            )
            pk[0, k, prow, :] = head
            pk[1, k, prow, :] = conduct
            stor[k, rows, :] = storage
            rhs[k, rows, :] = 2.0 * width * (sat_old[k, rows, :] - sq * sq)
            packed = jnp.where(pair_b == k, pltpu.roll(head, 2 * k + 1, 1), packed)
            packed = jnp.where(pair_b == k + 32, pltpu.roll(conduct, 2 * k + 65, 1), packed)
        ypack[1, rows, :] = packed
        return carry

    lax.fori_loop(0, RX // BLOCK, solve_first, 0)

    moves = halo_copies(1)
    for move in moves:
        move.start()
    lax.fori_loop(0, LAY, sideways, 0)
    halo_finish(1, moves)

    def solve_second(r, carry):
        rows = pl.ds(pl.multiple_of(r * BLOCK, BLOCK), BLOCK)
        prow = pl.ds(pl.multiple_of(r * BLOCK + 8, 8), BLOCK)
        head, conduct = pk[0, 0, prow, :], pk[1, 0, prow, :]
        v_prev = flux_prev = q_prev = last = None
        for k in range(LAY):
            comb = ycomb[rows, :]
            side_f = jnp.where(ends, pltpu.roll(comb, 127 - 2 * k, 1), 0.0)
            side_g = jnp.where(ends, pltpu.roll(comb, 63 - 2 * k, 1), 0.0)
            target = rhs[k, rows, :] - (lat[k, rows, :] + side_f)
            if k < ROOT:
                target = target - grid[k, rows, :]
            diag = stor[k, rows, :] + (gsum[k, rows, :] + side_g)
            if k < LAY - 1:
                head_n, conduct_n = pk[0, k + 1, prow, :], pk[1, k + 1, prow, :]
                v = 2.0 * (conduct + conduct_n)
                flux = v * (head - head_n + 1.0)
                diag = diag + v
                target = target - flux
            else:
                target = target - 4.0 * conduct
            if k > 0:
                target = target + flux_prev + v_prev * last
                diag = diag + v_prev - v_prev * q_prev
            else:
                target = target + grid[ROOT, rows, :]
            inv = 1.0 / diag
            last = target * inv
            val[k, rows, :] = last
            if k < LAY - 1:
                q_prev = v * inv
                upp[k, rows, :] = q_prev
                head, conduct, v_prev, flux_prev = head_n, conduct_n, v, flux
        numer = denom = jnp.zeros((BLOCK, 128), F32)
        for k in range(LAY - 1, -1, -1):
            if k < LAY - 1:
                last = val[k, rows, :] + upp[k, rows, :] * last
            head = pk[0, k, prow, :] + last
            val[k, rows, :] = head
            if k < ROOT:
                log_s = par_n[k, rows, :] * jnp.log2(
                    par_a[k, rows, :] * jnp.maximum(-head, TINY)
                )
                sat = jnp.exp2(-par_e[k, rows, :] * jnp.log2(1.0 + jnp.exp2(log_s)))
                weight = grid[k, rows, :]
                numer = numer + weight * sat
                denom = denom + weight
        state_ref[rows, :] = numer / jnp.maximum(denom, TINY)
        return carry

    lax.fori_loop(0, RX // BLOCK, solve_second, 0)
    out_copy = pltpu.make_async_copy(val, p_out, out_sem)
    out_copy.start()

    state = jnp.concatenate([state_ref[0:32, :], state_ref[32:64, :]], axis=1)
    s_hi = state.astype(BF16)
    left = state - s_hi.astype(F32)
    s_mid = left.astype(BF16)
    s_low = (left - s_mid.astype(F32)).astype(BF16)
    pieces = jnp.concatenate([s_hi, s_mid, s_low], axis=0)
    iota_r1 = lax.broadcasted_iota(I32, (32, 1024), 0)

    for g in sorted(range(GROUPS), key=lambda w: -WAVES[w]):
        got = lax.dot_general(
            pieces, b_mat[g], (((1,), (0,)), ((), ())), preferred_element_type=F32
        )
        got = got[0:32] + got[32:64] + got[64:96]
        line = jnp.sum(jnp.where(iota_r1 == row_of[g], got, 0.0), axis=0, keepdims=True)
        for j in range(PER):
            back[g * PER + j] = line[:, j * 128 : (j + 1) * 128]
        for target in TARGETS:
            spot = PLACE[target[0]]
            if spot // PER == g:
                pltpu.make_async_remote_copy(
                    back.at[spot], mine.at[me], ret_send, ret_recv,
                    device_id=peer(target), device_id_type=MESH,
                ).start()
    pltpu.make_async_copy(back.at[OWN], mine.at[me], ret_recv).start()
    pltpu.make_async_copy(mine, mine, ret_recv).wait()

    even, other = mine[pl.ds(0, 64, 2), 0, :], mine[pl.ds(1, 64, 2), 0, :]
    low_half = jnp.where(lane < 64, even, pltpu.roll(other, 64, 1))
    high_half = jnp.where(lane < 64, pltpu.roll(even, 64, 1), other)
    s_out[...] = jnp.where(lax.rem(me, 2) == 0, low_half, high_half)

    pltpu.make_async_copy(send.at[0 : PEERS - 1], send.at[0 : PEERS - 1], send_sem).wait()
    pltpu.make_async_copy(mine.at[0 : PEERS - 1], mine.at[0 : PEERS - 1], ret_send).wait()
    out_copy.wait()


def on_device(h_old, soil_type, ks_scale, soil_table, clump_brick, clump_cell, root_fraction,
              transpiration, infiltration):
    del clump_brick
    whole = lambda shape, dtype=F32: pltpu.VMEM(shape, dtype)
    cube = whole((LAY, RX, RY))
    dma = pltpu.SemaphoreType.DMA
    vmem = pl.BlockSpec(memory_space=pltpu.VMEM)
    hbm = pl.BlockSpec(memory_space=pl.ANY)
    scratch = [
        cube, whole((LAY, RX, RY), I32), cube,
        whole((1, SLOTS), I32), whole((ROOT, SLOTS)), whole((1, SLOTS)), whole((1, SLOTS)),
        whole((8, 128)), whole((8, SLOTS)), whole((PEERS, 8, 128)), whole((PEERS // 2, 2, 8, 128)),
        cube, cube, cube, cube, cube,
        whole((2, LAY, RX + 16, RY)), cube, cube, cube, cube,
        cube, cube, cube, cube, cube,
        whole((GROUPS, 256, 1024), BF16),
        whole((GROUPS, 1, 1024), I32), whole((FIELDS * 64, 256)), whole((FIELDS, RX, RY)),
        whole((2, RX, 128)), whole((2, 2, RX, 128)), whole((2, 2, 2, LAY, 8, 128)),
        whole((RX, 128)), whole((RX, 128)),
        whole((PEERS // 2, 1, 128)), whole((PEERS, 1, 128)),
        dma((7,)), dma, dma((GROUPS,)), dma((2, 4)), dma((2, 4)), dma, dma, dma,
    ]
    pressure, stress = pl.pallas_call(
        kernel,
        out_shape=(
            jax.ShapeDtypeStruct((LAY, RX, RY), F32),
            jax.ShapeDtypeStruct((PEERS // 2, 128), F32),
        ),
        in_specs=[hbm, hbm, hbm, vmem, hbm, hbm, hbm, hbm],
        out_specs=(hbm, vmem),
        scratch_shapes=scratch,
        compiler_params=pltpu.CompilerParams(
            collective_id=1, has_side_effects=True, vmem_limit_bytes=56 * 1024 * 1024
        ),
        name="step",
    )(
        h_old, soil_type, ks_scale, soil_table, clump_cell.reshape(1, SLOTS), root_fraction,
        transpiration.reshape(1, SLOTS), infiltration.reshape(1, SLOTS),
    )
    return pressure, stress.reshape(SLOTS)


def solution(mesh):
    cells = P(None, "bx", "by")
    slots = P(("bx", "by"))
    return jax.shard_map(
        on_device,
        mesh=mesh,
        in_specs=(cells, cells, cells, P(), slots, slots, P(None, ("bx", "by")), slots, slots),
        out_specs=(cells, slots),
        check_vma=False,
    )
```

```python
import itertools

import jax
import jax.numpy as jnp
from jax import lax
from jax.experimental import pallas as pl
from jax.experimental.pallas import tpu as pltpu
from jax.sharding import PartitionSpec as P

MESH = pl.DeviceIdType.MESH
NX, NY = 8, 16
PEERS = NX * NY
LAY, ROOT = 20, 14
RX, RY = 64, 128
SLOTS = RX * RY
FIELDS = ROOT + 1
BLOCK = 16
TINY = 1e-30
F32, BF16, I32 = jnp.float32, jnp.bfloat16, jnp.int32


def ring(d):
    return min(d, 4 - d)


PAIRS = sorted(
    itertools.product(range(4), range(2), range(4), range(2)),
    key=lambda o: (ring(o[0]) + ring(o[2]) + o[3], o[1], ring(o[0])),
)
GROUPS, PER = 8, 8
WAVES = (0, 1, 2, 3, 4, 5, 6, 7)
PLACE = {
    pair: wave * PER + i
    for wave, group in enumerate(WAVES)
    for i, pair in enumerate(PAIRS[group * PER : group * PER + PER])
}
OWN = PLACE[0, 0, 0, 0]
TARGETS = [
    (pair, b)
    for group in WAVES
    for pair in reversed(PAIRS[group * PER : group * PER + PER])
    for b in (1, 0)
    if any(pair) or b
]


def seen_back(pair):
    return PLACE[-pair[0] % 4, pair[1], -pair[2] % 4, pair[3]]


def closures(head, alpha, shape_n, exponent, ks, width):
    log_s = shape_n * jnp.log2(alpha * jnp.maximum(-head, TINY))
    log_b = jnp.log2(1.0 + jnp.exp2(log_s))
    log_w = exponent * (log_s - log_b)
    root = jnp.exp2(-0.5 * exponent * log_b)
    inner = 1.0 - jnp.exp2(log_w)
    conduct = ks * root * (inner * inner)
    storage = 0.4 + 2.0 * width * (shape_n - 1.0) * alpha * jnp.exp2(log_w - log_b)
    return root, conduct, storage


def kernel(
    h_hbm, soil_hbm, ks_hbm, table_ref, cell_hbm, root_hbm, transp_hbm, infil_hbm,
    p_out, s_out,
    h, soil, ks_in, cell, root, transp, infil,
    table, fields1, send, recv,
    par_a, par_n, par_e, par_k, par_w,
    pk, sat_old, stor, lat, gsum,
    rinv, low, upp, rhs, val,
    b_mat, row_of, acc, grid,
    ypack, yrecv, xrecv, ycomb, state_ref,
    back, mine,
    in_sem, send_sem, recv_sem, halo_send, halo_recv, ret_send, ret_recv, out_sem,
):
    bx = lax.axis_index("bx")
    by = lax.axis_index("by")
    me = bx * NY + by

    copies = [
        pltpu.make_async_copy(src, dst, in_sem.at[i])
        for i, (src, dst) in enumerate(
            (
                (root_hbm, root), (transp_hbm, transp), (infil_hbm, infil), (cell_hbm, cell),
                (h_hbm, h), (soil_hbm, soil), (ks_hbm, ks_in),
            )
        )
    ]
    for copy in copies:
        copy.start()

    core = lax.rem(bx, 2)
    cores = (core, 1 - core)
    ys = [lax.rem(bx // 2 + d, 4) * 2 for d in range(4)]
    xs = [lax.rem(by // 4 + d, 4) * 4 for d in range(4)]
    half = lax.rem(by, 2)
    halves = (half, 1 - half)
    upper = lax.rem(by, 4) - half
    zs = (upper, 2 - upper)

    def peer(target):
        (y, c, x, z), b = target
        return ys[y] + cores[c], xs[x] + zs[z] + halves[b]

    barrier = pltpu.get_barrier_semaphore()
    for target in TARGETS:
        pl.semaphore_signal(barrier, inc=1, device_id=peer(target), device_id_type=MESH)

    lane8 = lax.broadcasted_iota(I32, (8, 128), 1)
    sub8 = lax.broadcasted_iota(I32, (8, 128), 0)
    first_half = lane8 < 64

    for copy in copies[:4]:
        copy.wait()
    fields1[0:6, :] = root[8:14, :]
    fields1[6:7, :] = infil[...]
    fields1[7:8, :] = cell[...].astype(F32)

    def pack(q, carry):
        at = pl.ds(pl.multiple_of(q * 128, 128), 128)
        demand = transp[:, at]
        v0 = root[0:8, at] * demand
        v1 = fields1[:, at] * jnp.where(sub8 < 6, demand, 1.0)
        r0 = pltpu.roll(v0, 64, 1)
        r1 = pltpu.roll(v1, 64, 1)
        send[2 * q] = jnp.where(first_half, v0, r1)
        send[2 * q + 1] = jnp.where(first_half, r0, v1)
        return carry

    lax.fori_loop(0, PEERS // 2, pack, 0, unroll=8)

    table[...] = jnp.zeros_like(table)
    table[0:4, 0:12] = table_ref[...]
    for copy in copies[4:]:
        copy.wait()
    t0, t1, t2, t3 = (jnp.broadcast_to(table[i : i + 1, :], (RX, 128)) for i in range(4))
    lane = lax.broadcasted_iota(I32, (RX, 128), 1)

    def first(k, packed):
        kind = soil[k]
        look = lambda t: jnp.take_along_axis(t, kind, axis=1, mode="promise_in_bounds")
        alpha = 4.0 * look(t0)
        shape_n = 1.2 + 2.0 * look(t1)
        ks = 0.75 * look(t2) * ks_in[k]
        width = 0.25 + 0.3 * look(t3)
        exponent = 1.0 - 1.0 / shape_n
        par_a[k], par_n[k], par_e[k], par_k[k], par_w[k] = alpha, shape_n, exponent, ks, width
        head = h[k]
        sq, conduct, storage = closures(head, alpha, shape_n, exponent, ks, width)
        sat_old[k] = sq * sq
        stor[k] = storage
        pk[0, k, 8 : 8 + RX, :] = head
        pk[1, k, 8 : 8 + RX, :] = conduct
        turn = 2 * k + 1
        pair = lane // 2
        packed = jnp.where(pair == k, pltpu.roll(head, turn, 1), packed)
        packed = jnp.where(pair == k + 32, pltpu.roll(conduct, turn + 64, 1), packed)
        return packed

    ypack[0] = lax.fori_loop(0, LAY, first, jnp.zeros((RX, 128), F32))

    pl.semaphore_wait(barrier, PEERS - 1)

    def halo_copies(step):
        up = lax.rem(bx + NX - 1, NX), by
        down = lax.rem(bx + 1, NX), by
        left = bx, lax.rem(by + NY - 1, NY)
        right = bx, lax.rem(by + 1, NY)
        moves = (
            (pk.at[:, :, pl.ds(71, 1), :], xrecv.at[step, 0, :, :, pl.ds(0, 1), :], down),
            (pk.at[:, :, pl.ds(8, 1), :], xrecv.at[step, 1, :, :, pl.ds(7, 1), :], up),
            (ypack.at[step], yrecv.at[step, 0], right),
            (ypack.at[step], yrecv.at[step, 1], left),
        )
        return [
            pltpu.make_async_remote_copy(
                src, dst, halo_send.at[step, i], halo_recv.at[step, i],
                device_id=to, device_id_type=MESH,
            )
            for i, (src, dst, to) in enumerate(moves)
        ]

    odd = lax.rem(lane, 2) == 1
    lane_b = lax.broadcasted_iota(I32, (BLOCK, 128), 1)
    pair_b = lane_b // 2

    def halo_finish(step, moves):
        for move in moves:
            move.wait_recv()
        for move in moves:
            move.wait_send()
        own = ypack[step]
        both = jnp.where(
            odd, pltpu.roll(yrecv[step, 0], 1, 1), pltpu.roll(yrecv[step, 1], 127, 1)
        )
        edge = jnp.logical_or(
            jnp.logical_and(odd, by == 0), jnp.logical_and(jnp.logical_not(odd), by == NY - 1)
        )
        both = jnp.where(edge, -own, both)
        face = pltpu.roll(own + both, 64, 1)
        flow = face * (own - both)
        ycomb[...] = jnp.where(lane < 64, flow, own + both)
        for side, row, off in ((0, 0, bx == 0), (1, 7, bx == NX - 1)):
            tile = pl.ds(side * (RX - 8), 8)
            owned = pl.ds(side * (RX - 8) + 8, 8)
            here = sub8 == row
            for k in range(LAY):
                k_own = pk[1, k, owned, :]
                g = k_own + jnp.where(off, -k_own, xrecv[step, side, 1, k])
                f = g * (pk[0, k, owned, :] - xrecv[step, side, 0, k])
                gsum[k, tile, :] += jnp.where(here, g, 0.0)
                lat[k, tile, :] += jnp.where(here, f, 0.0)

    at_first = lane == 0

    def sideways(k, carry):
        head, conduct = pk[0, k, 8:72, :], pk[1, k, 8:72, :]
        g = jnp.where(at_first, 0.0, conduct + pltpu.roll(conduct, 1, 1))
        f = g * (head - pltpu.roll(head, 1, 1))
        gx = conduct[:-1] + conduct[1:]
        fx = gx * (head[1:] - head[:-1])
        zero = jnp.zeros((1, 128), F32)
        gx0 = jnp.concatenate([zero, gx], axis=0)
        gx1 = jnp.concatenate([gx, zero], axis=0)
        fx0 = jnp.concatenate([zero, fx], axis=0)
        fx1 = jnp.concatenate([fx, zero], axis=0)
        gsum[k] = (g + pltpu.roll(g, 127, 1)) + (gx0 + gx1)
        lat[k] = (f - pltpu.roll(f, 127, 1)) + (fx0 - fx1)
        return carry

    moves = halo_copies(0)
    for move in moves:
        move.start()

    pltpu.make_async_copy(send.at[me], recv.at[OWN, half], recv_sem.at[OWN // PER]).start()
    for target in TARGETS:
        tx, ty = peer(target)
        spot = seen_back(target[0])
        pltpu.make_async_remote_copy(
            send.at[tx * NY + ty], recv.at[spot, half], send_sem, recv_sem.at[spot // PER],
            device_id=(tx, ty), device_id_type=MESH,
        ).start()

    lax.fori_loop(0, LAY, sideways, 0)
    iota_c = lax.broadcasted_iota(I32, (256, 128), 0)
    iota_r = lax.broadcasted_iota(I32, (32, 128), 0)
    acc[...] = jnp.zeros_like(acc)

    def spread_tile(g, j):
        m0, m1 = recv[g * PER + j, 0], recv[g * PER + j, 1]
        v0 = jnp.where(first_half, m0, pltpu.roll(m1, 64, 1))
        v1 = jnp.where(first_half, pltpu.roll(m0, 64, 1), m1)
        at = slice(j * 128, (j + 1) * 128)
        spot = v1[7:8, :].astype(I32)
        brow = spot >> 7
        col = (spot & 127) + ((brow >> 5) << 7)
        brow = brow & 31
        row_of[g, :, at] = brow
        b_mat[g, :, at] = jnp.where(iota_c == col, 1.0, 0.0).astype(BF16)
        hit = iota_r == brow
        spread = lambda line: jnp.where(hit, line, 0.0).astype(BF16)
        h0 = v0.astype(BF16).astype(F32)
        h1 = v1.astype(BF16).astype(F32)
        pieces = []
        for f in range(FIELDS):
            high, whole = (h0, v0) if f < 8 else (h1, v1)
            row = slice(f % 8, f % 8 + 1)
            pieces.append(spread(high[row]))
            pieces.append(spread((whole - high)[row]))
        return jnp.concatenate(pieces, axis=0)

    def place(g, carry):
        part_of = recv.at[pl.ds(g * PER, PER)]
        pltpu.make_async_copy(part_of, part_of, recv_sem.at[g]).wait()
        for part in range(PER // 2):
            blocks = []
            for j in range(part * 2, part * 2 + 2):
                blocks.append(spread_tile(g, j))
            a_val = jnp.concatenate(blocks, axis=1) if len(blocks) > 1 else blocks[0]
            acc[...] += lax.dot_general(
                a_val, b_mat[g, :, part * 256 : part * 256 + 256], (((1,), (1,)), ((), ())),
                preferred_element_type=F32,
            )
        return carry

    halo_finish(0, moves)
    ends = jnp.logical_or(lane_b == 0, lane_b == 127)

    def factor_first(r, carry):
        rows = pl.ds(pl.multiple_of(r * BLOCK, BLOCK), BLOCK)
        prow = pl.ds(pl.multiple_of(r * BLOCK + 8, 8), BLOCK)
        head, conduct = pk[0, 0, prow, :], pk[1, 0, prow, :]
        v_prev = flux_prev = q_prev = None
        for k in range(LAY):
            comb = ycomb[rows, :]
            side_f = jnp.where(ends, pltpu.roll(comb, 127 - 2 * k, 1), 0.0)
            side_g = jnp.where(ends, pltpu.roll(comb, 63 - 2 * k, 1), 0.0)
            target = -(lat[k, rows, :] + side_f)
            diag = stor[k, rows, :] + (gsum[k, rows, :] + side_g)
            if k < LAY - 1:
                head_n, conduct_n = pk[0, k + 1, prow, :], pk[1, k + 1, prow, :]
                v = 2.0 * (conduct + conduct_n)
                flux = v * (head - head_n + 1.0)
                diag = diag + v
                target = target - flux
            else:
                target = target - 4.0 * conduct
            if k > 0:
                target = target + flux_prev
                diag = diag + v_prev - v_prev * q_prev
            inv = 1.0 / diag
            rinv[k, rows, :] = inv
            rhs[k, rows, :] = target * inv
            if k > 0:
                low[k, rows, :] = v_prev * inv
            if k < LAY - 1:
                q_prev = v * inv
                upp[k, rows, :] = q_prev
                head, conduct, v_prev, flux_prev = head_n, conduct_n, v, flux
        return carry

    lax.fori_loop(0, RX // BLOCK, factor_first, 0)
    lax.fori_loop(0, GROUPS, place, 0)

    for f in range(FIELDS):
        both = acc[f * 64 : f * 64 + 32, :] + acc[f * 64 + 32 : f * 64 + 64, :]
        grid[f, 0:32, :] = both[:, :128]
        grid[f, 32:64, :] = both[:, 128:]
    def solve_first(r, carry):
        rows = pl.ds(pl.multiple_of(r * BLOCK, BLOCK), BLOCK)
        prow = pl.ds(pl.multiple_of(r * BLOCK + 8, 8), BLOCK)
        last = rhs[0, rows, :] + (grid[ROOT, rows, :] - grid[0, rows, :]) * rinv[0, rows, :]
        val[0, rows, :] = last
        for k in range(1, LAY):
            here = rhs[k, rows, :]
            if k < ROOT:
                here = here - grid[k, rows, :] * rinv[k, rows, :]
            last = here + low[k, rows, :] * last
            val[k, rows, :] = last
        packed = jnp.zeros((BLOCK, 128), F32)
        for k in range(LAY - 1, -1, -1):
            if k < LAY - 1:
                last = val[k, rows, :] + upp[k, rows, :] * last
            head = pk[0, k, prow, :] + last
            width = par_w[k, rows, :]
            sq, conduct, storage = closures(
                head, par_a[k, rows, :], par_n[k, rows, :], par_e[k, rows, :],
                par_k[k, rows, :], width,
            )
            pk[0, k, prow, :] = head
            pk[1, k, prow, :] = conduct
            stor[k, rows, :] = storage
            rhs[k, rows, :] = 2.0 * width * (sat_old[k, rows, :] - sq * sq)
            packed = jnp.where(pair_b == k, pltpu.roll(head, 2 * k + 1, 1), packed)
            packed = jnp.where(pair_b == k + 32, pltpu.roll(conduct, 2 * k + 65, 1), packed)
        ypack[1, rows, :] = packed
        return carry

    lax.fori_loop(0, RX // BLOCK, solve_first, 0)

    moves = halo_copies(1)
    for move in moves:
        move.start()
    lax.fori_loop(0, LAY, sideways, 0)
    halo_finish(1, moves)

    def solve_second(r, carry):
        rows = pl.ds(pl.multiple_of(r * BLOCK, BLOCK), BLOCK)
        prow = pl.ds(pl.multiple_of(r * BLOCK + 8, 8), BLOCK)
        head, conduct = pk[0, 0, prow, :], pk[1, 0, prow, :]
        v_prev = flux_prev = q_prev = last = None
        for k in range(LAY):
            comb = ycomb[rows, :]
            side_f = jnp.where(ends, pltpu.roll(comb, 127 - 2 * k, 1), 0.0)
            side_g = jnp.where(ends, pltpu.roll(comb, 63 - 2 * k, 1), 0.0)
            target = rhs[k, rows, :] - (lat[k, rows, :] + side_f)
            if k < ROOT:
                target = target - grid[k, rows, :]
            diag = stor[k, rows, :] + (gsum[k, rows, :] + side_g)
            if k < LAY - 1:
                head_n, conduct_n = pk[0, k + 1, prow, :], pk[1, k + 1, prow, :]
                v = 2.0 * (conduct + conduct_n)
                flux = v * (head - head_n + 1.0)
                diag = diag + v
                target = target - flux
            else:
                target = target - 4.0 * conduct
            if k > 0:
                target = target + flux_prev + v_prev * last
                diag = diag + v_prev - v_prev * q_prev
            else:
                target = target + grid[ROOT, rows, :]
            inv = 1.0 / diag
            last = target * inv
            val[k, rows, :] = last
            if k < LAY - 1:
                q_prev = v * inv
                upp[k, rows, :] = q_prev
                head, conduct, v_prev, flux_prev = head_n, conduct_n, v, flux
        numer = denom = jnp.zeros((BLOCK, 128), F32)
        for k in range(LAY - 1, -1, -1):
            if k < LAY - 1:
                last = val[k, rows, :] + upp[k, rows, :] * last
            head = pk[0, k, prow, :] + last
            val[k, rows, :] = head
            if k < ROOT:
                log_s = par_n[k, rows, :] * jnp.log2(
                    par_a[k, rows, :] * jnp.maximum(-head, TINY)
                )
                sat = jnp.exp2(-par_e[k, rows, :] * jnp.log2(1.0 + jnp.exp2(log_s)))
                weight = grid[k, rows, :]
                numer = numer + weight * sat
                denom = denom + weight
        state_ref[rows, :] = numer / jnp.maximum(denom, TINY)
        return carry

    lax.fori_loop(0, RX // BLOCK, solve_second, 0)
    out_copy = pltpu.make_async_copy(val, p_out, out_sem)
    out_copy.start()

    state = jnp.concatenate([state_ref[0:32, :], state_ref[32:64, :]], axis=1)
    s_hi = state.astype(BF16)
    left = state - s_hi.astype(F32)
    s_mid = left.astype(BF16)
    s_low = (left - s_mid.astype(F32)).astype(BF16)
    pieces = jnp.concatenate([s_hi, s_mid, s_low], axis=0)
    iota_r1 = lax.broadcasted_iota(I32, (32, 1024), 0)

    for g in sorted(range(GROUPS), key=lambda w: -WAVES[w]):
        got = lax.dot_general(
            pieces, b_mat[g], (((1,), (0,)), ((), ())), preferred_element_type=F32
        )
        got = got[0:32] + got[32:64] + got[64:96]
        line = jnp.sum(jnp.where(iota_r1 == row_of[g], got, 0.0), axis=0, keepdims=True)
        for j in range(PER):
            back[g * PER + j] = line[:, j * 128 : (j + 1) * 128]
        for target in TARGETS:
            spot = PLACE[target[0]]
            if spot // PER == g:
                pltpu.make_async_remote_copy(
                    back.at[spot], mine.at[me], ret_send, ret_recv,
                    device_id=peer(target), device_id_type=MESH,
                ).start()
    pltpu.make_async_copy(back.at[OWN], mine.at[me], ret_recv).start()
    pltpu.make_async_copy(mine, mine, ret_recv).wait()

    even, other = mine[pl.ds(0, 64, 2), 0, :], mine[pl.ds(1, 64, 2), 0, :]
    low_half = jnp.where(lane < 64, even, pltpu.roll(other, 64, 1))
    high_half = jnp.where(lane < 64, pltpu.roll(even, 64, 1), other)
    s_out[...] = jnp.where(lax.rem(me, 2) == 0, low_half, high_half)

    pltpu.make_async_copy(send.at[0 : PEERS - 1], send.at[0 : PEERS - 1], send_sem).wait()
    pltpu.make_async_copy(mine.at[0 : PEERS - 1], mine.at[0 : PEERS - 1], ret_send).wait()
    out_copy.wait()


def deliver(p_in, s_in, p_out, s_out, held, line, sem_in, sem_out):
    steps = [
        (p_in.at[pl.ds(k, 4)], held.at[pl.ds(k, 4)], p_out.at[pl.ds(k, 4)]) for k in range(0, LAY, 4)
    ]
    steps.append((s_in, line, s_out))
    reads = [
        pltpu.make_async_copy(a, b, sem_in.at[i]) for i, (a, b, _) in enumerate(steps)
    ]
    writes = [
        pltpu.make_async_copy(b, c, sem_out.at[i]) for i, (_, b, c) in enumerate(steps)
    ]
    for read in reads:
        read.start()
    for read, write in zip(reads, writes):
        read.wait()
        write.start()
    for write in writes:
        write.wait()


def on_device(h_old, soil_type, ks_scale, soil_table, clump_brick, clump_cell, root_fraction,
              transpiration, infiltration):
    del clump_brick
    whole = lambda shape, dtype=F32: pltpu.VMEM(shape, dtype)
    cube = whole((LAY, RX, RY))
    dma = pltpu.SemaphoreType.DMA
    vmem = pl.BlockSpec(memory_space=pltpu.VMEM)
    hbm = pl.BlockSpec(memory_space=pl.ANY)
    scratch = [
        cube, whole((LAY, RX, RY), I32), cube,
        whole((1, SLOTS), I32), whole((ROOT, SLOTS)), whole((1, SLOTS)), whole((1, SLOTS)),
        whole((8, 128)), whole((8, SLOTS)), whole((PEERS, 8, 128)), whole((PEERS // 2, 2, 8, 128)),
        cube, cube, cube, cube, cube,
        whole((2, LAY, RX + 16, RY)), cube, cube, cube, cube,
        cube, cube, cube, cube, cube,
        whole((GROUPS, 256, 1024), BF16),
        whole((GROUPS, 1, 1024), I32), whole((FIELDS * 64, 256)), whole((FIELDS, RX, RY)),
        whole((2, RX, 128)), whole((2, 2, RX, 128)), whole((2, 2, 2, LAY, 8, 128)),
        whole((RX, 128)), whole((RX, 128)),
        whole((PEERS // 2, 1, 128)), whole((PEERS, 1, 128)),
        dma((7,)), dma, dma((GROUPS,)), dma((2, 4)), dma((2, 4)), dma, dma, dma,
    ]
    pressure, stress = pl.pallas_call(
        kernel,
        out_shape=(
            jax.ShapeDtypeStruct((LAY, RX, RY), F32),
            jax.ShapeDtypeStruct((PEERS // 2, 128), F32),
        ),
        in_specs=[hbm, hbm, hbm, vmem, hbm, hbm, hbm, hbm],
        out_specs=(hbm, vmem),
        scratch_shapes=scratch,
        compiler_params=pltpu.CompilerParams(
            collective_id=1, has_side_effects=True, vmem_limit_bytes=56 * 1024 * 1024
        ),
        name="step",
    )(
        h_old, soil_type, ks_scale, soil_table, clump_cell.reshape(1, SLOTS), root_fraction,
        transpiration.reshape(1, SLOTS), infiltration.reshape(1, SLOTS),
    )
    pressure, stress = pl.pallas_call(
        deliver,
        out_shape=(
            jax.ShapeDtypeStruct((LAY, RX, RY), F32),
            jax.ShapeDtypeStruct((PEERS // 2, 128), F32),
        ),
        in_specs=[hbm, hbm],
        out_specs=(hbm, hbm),
        scratch_shapes=[cube, whole((PEERS // 2, 128)), dma((6,)), dma((6,))],
        name="deliver",
    )(pressure, stress)
    return pressure, stress.reshape(SLOTS)


def solution(mesh):
    cells = P(None, "bx", "by")
    slots = P(("bx", "by"))
    return jax.shard_map(
        on_device,
        mesh=mesh,
        in_specs=(cells, cells, cells, P(), slots, slots, P(None, ("bx", "by")), slots, slots),
        out_specs=(cells, slots),
        check_vma=False,
    )
```

```python
import itertools

import jax
import jax.numpy as jnp
from jax import lax
from jax.experimental import pallas as pl
from jax.experimental.pallas import tpu as pltpu
from jax.sharding import PartitionSpec as P

MESH = pl.DeviceIdType.MESH
NX, NY = 8, 16
PEERS = NX * NY
LAY, ROOT = 20, 14
RX, RY = 64, 128
SLOTS = RX * RY
FIELDS = ROOT + 1
BLOCK = 16
TINY = 1e-30
F32, BF16, I32 = jnp.float32, jnp.bfloat16, jnp.int32
F8 = jnp.float8_e4m3fn


def ring(d):
    return min(d, 4 - d)


PAIRS = sorted(
    itertools.product(range(4), range(2), range(4), range(2)),
    key=lambda o: (ring(o[0]) + ring(o[2]) + o[3], o[1], ring(o[0])),
)
GROUPS, PER = 8, 8
WAVES = (0, 1, 2, 3, 4, 5, 6, 7)
PLACE = {
    pair: wave * PER + i
    for wave, group in enumerate(WAVES)
    for i, pair in enumerate(PAIRS[group * PER : group * PER + PER])
}
OWN = PLACE[0, 0, 0, 0]
TARGETS = [
    (pair, b)
    for group in WAVES
    for pair in reversed(PAIRS[group * PER : group * PER + PER])
    for b in (1, 0)
    if any(pair) or b
]


def seen_back(pair):
    return PLACE[-pair[0] % 4, pair[1], -pair[2] % 4, pair[3]]


def closures(head, alpha, shape_n, exponent, ks, width):
    log_s = shape_n * jnp.log2(alpha * jnp.maximum(-head, TINY))
    log_b = jnp.log2(1.0 + jnp.exp2(log_s))
    log_w = exponent * (log_s - log_b)
    root = jnp.exp2(-0.5 * exponent * log_b)
    inner = 1.0 - jnp.exp2(log_w)
    conduct = ks * root * (inner * inner)
    storage = 0.4 + 2.0 * width * (shape_n - 1.0) * alpha * jnp.exp2(log_w - log_b)
    return root, conduct, storage


def kernel(
    h_hbm, soil_hbm, ks_hbm, table_ref, cell_hbm, root_hbm, transp_hbm, infil_hbm,
    p_out, s_out,
    h, soil, ks_in, cell, root, transp, infil,
    table, fields1, send, recv,
    par_a, par_n, par_e, par_k, par_w,
    pk, sat_old, stor, lat, gsum,
    rinv, low, upp, rhs, val,
    b_mat, row_of, acc, grid,
    ypack, yrecv, xrecv, ycomb, state_ref,
    back, mine,
    in_sem, send_sem, recv_sem, halo_send, halo_recv, ret_send, ret_recv, out_sem,
):
    bx = lax.axis_index("bx")
    by = lax.axis_index("by")
    me = bx * NY + by

    copies = [
        pltpu.make_async_copy(src, dst, in_sem.at[i])
        for i, (src, dst) in enumerate(
            (
                (root_hbm, root), (transp_hbm, transp), (infil_hbm, infil), (cell_hbm, cell),
                (h_hbm, h), (soil_hbm, soil), (ks_hbm, ks_in),
            )
        )
    ]
    for copy in copies:
        copy.start()

    core = lax.rem(bx, 2)
    cores = (core, 1 - core)
    ys = [lax.rem(bx // 2 + d, 4) * 2 for d in range(4)]
    xs = [lax.rem(by // 4 + d, 4) * 4 for d in range(4)]
    half = lax.rem(by, 2)
    halves = (half, 1 - half)
    upper = lax.rem(by, 4) - half
    zs = (upper, 2 - upper)

    def peer(target):
        (y, c, x, z), b = target
        return ys[y] + cores[c], xs[x] + zs[z] + halves[b]

    barrier = pltpu.get_barrier_semaphore()
    for target in TARGETS:
        pl.semaphore_signal(barrier, inc=1, device_id=peer(target), device_id_type=MESH)

    lane8 = lax.broadcasted_iota(I32, (8, 128), 1)
    sub8 = lax.broadcasted_iota(I32, (8, 128), 0)
    first_half = lane8 < 64

    for copy in copies[:4]:
        copy.wait()
    fields1[0:6, :] = root[8:14, :]
    fields1[6:7, :] = infil[...]
    fields1[7:8, :] = cell[...].astype(F32)

    def pack(q, carry):
        at = pl.ds(pl.multiple_of(q * 128, 128), 128)
        demand = transp[:, at]
        v0 = root[0:8, at] * demand
        v1 = fields1[:, at] * jnp.where(sub8 < 6, demand, 1.0)
        r0 = pltpu.roll(v0, 64, 1)
        r1 = pltpu.roll(v1, 64, 1)
        send[2 * q] = jnp.where(first_half, v0, r1)
        send[2 * q + 1] = jnp.where(first_half, r0, v1)
        return carry

    lax.fori_loop(0, PEERS // 2, pack, 0, unroll=8)

    table[...] = jnp.zeros_like(table)
    table[0:4, 0:12] = table_ref[...]
    for copy in copies[4:]:
        copy.wait()
    t0, t1, t2, t3 = (jnp.broadcast_to(table[i : i + 1, :], (RX, 128)) for i in range(4))
    lane = lax.broadcasted_iota(I32, (RX, 128), 1)

    def first(k, packed):
        kind = soil[k]
        look = lambda t: jnp.take_along_axis(t, kind, axis=1, mode="promise_in_bounds")
        alpha = 4.0 * look(t0)
        shape_n = 1.2 + 2.0 * look(t1)
        ks = 0.75 * look(t2) * ks_in[k]
        width = 0.25 + 0.3 * look(t3)
        exponent = 1.0 - 1.0 / shape_n
        par_a[k], par_n[k], par_e[k], par_k[k], par_w[k] = alpha, shape_n, exponent, ks, width
        head = h[k]
        sq, conduct, storage = closures(head, alpha, shape_n, exponent, ks, width)
        sat_old[k] = sq * sq
        stor[k] = storage
        pk[0, k, 8 : 8 + RX, :] = head
        pk[1, k, 8 : 8 + RX, :] = conduct
        turn = 2 * k + 1
        pair = lane // 2
        packed = jnp.where(pair == k, pltpu.roll(head, turn, 1), packed)
        packed = jnp.where(pair == k + 32, pltpu.roll(conduct, turn + 64, 1), packed)
        return packed

    ypack[0] = lax.fori_loop(0, LAY, first, jnp.zeros((RX, 128), F32))

    pl.semaphore_wait(barrier, PEERS - 1)

    def halo_copies(step):
        up = lax.rem(bx + NX - 1, NX), by
        down = lax.rem(bx + 1, NX), by
        left = bx, lax.rem(by + NY - 1, NY)
        right = bx, lax.rem(by + 1, NY)
        moves = (
            (pk.at[:, :, pl.ds(71, 1), :], xrecv.at[step, 0, :, :, pl.ds(0, 1), :], down),
            (pk.at[:, :, pl.ds(8, 1), :], xrecv.at[step, 1, :, :, pl.ds(7, 1), :], up),
            (ypack.at[step], yrecv.at[step, 0], right),
            (ypack.at[step], yrecv.at[step, 1], left),
        )
        return [
            pltpu.make_async_remote_copy(
                src, dst, halo_send.at[step, i], halo_recv.at[step, i],
                device_id=to, device_id_type=MESH,
            )
            for i, (src, dst, to) in enumerate(moves)
        ]

    odd = lax.rem(lane, 2) == 1
    lane_b = lax.broadcasted_iota(I32, (BLOCK, 128), 1)
    pair_b = lane_b // 2

    def halo_finish(step, moves):
        for move in moves:
            move.wait_recv()
        for move in moves:
            move.wait_send()
        own = ypack[step]
        both = jnp.where(
            odd, pltpu.roll(yrecv[step, 0], 1, 1), pltpu.roll(yrecv[step, 1], 127, 1)
        )
        edge = jnp.logical_or(
            jnp.logical_and(odd, by == 0), jnp.logical_and(jnp.logical_not(odd), by == NY - 1)
        )
        both = jnp.where(edge, -own, both)
        face = pltpu.roll(own + both, 64, 1)
        flow = face * (own - both)
        ycomb[...] = jnp.where(lane < 64, flow, own + both)
        for side, row, off in ((0, 0, bx == 0), (1, 7, bx == NX - 1)):
            tile = pl.ds(side * (RX - 8), 8)
            owned = pl.ds(side * (RX - 8) + 8, 8)
            here = sub8 == row
            for k in range(LAY):
                k_own = pk[1, k, owned, :]
                g = k_own + jnp.where(off, -k_own, xrecv[step, side, 1, k])
                f = g * (pk[0, k, owned, :] - xrecv[step, side, 0, k])
                gsum[k, tile, :] += jnp.where(here, g, 0.0)
                lat[k, tile, :] += jnp.where(here, f, 0.0)

    at_first = lane == 0

    def sideways(k, carry):
        head, conduct = pk[0, k, 8:72, :], pk[1, k, 8:72, :]
        g = jnp.where(at_first, 0.0, conduct + pltpu.roll(conduct, 1, 1))
        f = g * (head - pltpu.roll(head, 1, 1))
        gx = conduct[:-1] + conduct[1:]
        fx = gx * (head[1:] - head[:-1])
        zero = jnp.zeros((1, 128), F32)
        gx0 = jnp.concatenate([zero, gx], axis=0)
        gx1 = jnp.concatenate([gx, zero], axis=0)
        fx0 = jnp.concatenate([zero, fx], axis=0)
        fx1 = jnp.concatenate([fx, zero], axis=0)
        gsum[k] = (g + pltpu.roll(g, 127, 1)) + (gx0 + gx1)
        lat[k] = (f - pltpu.roll(f, 127, 1)) + (fx0 - fx1)
        return carry

    moves = halo_copies(0)
    for move in moves:
        move.start()

    pltpu.make_async_copy(send.at[me], recv.at[OWN, half], recv_sem.at[OWN // PER]).start()
    for target in TARGETS:
        tx, ty = peer(target)
        spot = seen_back(target[0])
        pltpu.make_async_remote_copy(
            send.at[tx * NY + ty], recv.at[spot, half], send_sem, recv_sem.at[spot // PER],
            device_id=(tx, ty), device_id_type=MESH,
        ).start()

    lax.fori_loop(0, LAY, sideways, 0)
    iota_c = lax.broadcasted_iota(I32, (256, 128), 0)
    iota_r = lax.broadcasted_iota(I32, (32, 128), 0)
    acc[...] = jnp.zeros_like(acc)

    def spread_tile(g, j):
        m0, m1 = recv[g * PER + j, 0], recv[g * PER + j, 1]
        v0 = jnp.where(first_half, m0, pltpu.roll(m1, 64, 1))
        v1 = jnp.where(first_half, pltpu.roll(m0, 64, 1), m1)
        at = slice(j * 128, (j + 1) * 128)
        spot = v1[7:8, :].astype(I32)
        brow = spot >> 7
        col = (spot & 127) + ((brow >> 5) << 7)
        brow = brow & 31
        row_of[g, :, at] = brow
        b_mat[g, :, at] = jnp.where(iota_c == col, 1.0, 0.0).astype(BF16)
        hit = iota_r == brow
        spread = lambda line: jnp.where(hit, line, 0.0).astype(BF16)
        fine = lambda line: jnp.where(hit, line, 0.0).astype(F8)
        h0 = v0.astype(BF16).astype(F32)
        h1 = v1.astype(BF16).astype(F32)
        high, low_part = [], []
        for f in range(FIELDS):
            top, whole_v = (h0, v0) if f < 8 else (h1, v1)
            row = slice(f % 8, f % 8 + 1)
            high.append(spread(top[row]))
            if f < ROOT:
                low_part.append(fine(((whole_v - top) * 32768.0)[row]))
        high.append(spread((v1 - h1)[6:7]))
        cols = jnp.where(iota_c == col, 1.0, 0.0).astype(F8)
        return jnp.concatenate(high, axis=0), jnp.concatenate(low_part, axis=0), cols

    def place(g, carry):
        part_of = recv.at[pl.ds(g * PER, PER)]
        pltpu.make_async_copy(part_of, part_of, recv_sem.at[g]).wait()
        for part in range(PER // 2):
            blocks = [spread_tile(g, j) for j in range(part * 2, part * 2 + 2)]
            high, low_part, cols = (jnp.concatenate(b, axis=1) for b in zip(*blocks))
            dims = (((1,), (1,)), ((), ()))
            acc[0 : FIELDS * 32 + 32] += lax.dot_general(
                high, b_mat[g, :, part * 256 : part * 256 + 256], dims, preferred_element_type=F32
            )
            acc[FIELDS * 32 + 32 : FIELDS * 64] += lax.dot_general(
                low_part, cols, dims, preferred_element_type=F32
            )
        return carry

    halo_finish(0, moves)
    ends = jnp.logical_or(lane_b == 0, lane_b == 127)

    def factor_first(r, carry):
        rows = pl.ds(pl.multiple_of(r * BLOCK, BLOCK), BLOCK)
        prow = pl.ds(pl.multiple_of(r * BLOCK + 8, 8), BLOCK)
        head, conduct = pk[0, 0, prow, :], pk[1, 0, prow, :]
        v_prev = flux_prev = q_prev = None
        for k in range(LAY):
            comb = ycomb[rows, :]
            side_f = jnp.where(ends, pltpu.roll(comb, 127 - 2 * k, 1), 0.0)
            side_g = jnp.where(ends, pltpu.roll(comb, 63 - 2 * k, 1), 0.0)
            target = -(lat[k, rows, :] + side_f)
            diag = stor[k, rows, :] + (gsum[k, rows, :] + side_g)
            if k < LAY - 1:
                head_n, conduct_n = pk[0, k + 1, prow, :], pk[1, k + 1, prow, :]
                v = 2.0 * (conduct + conduct_n)
                flux = v * (head - head_n + 1.0)
                diag = diag + v
                target = target - flux
            else:
                target = target - 4.0 * conduct
            if k > 0:
                target = target + flux_prev
                diag = diag + v_prev - v_prev * q_prev
            inv = 1.0 / diag
            rinv[k, rows, :] = inv
            rhs[k, rows, :] = target * inv
            if k > 0:
                low[k, rows, :] = v_prev * inv
            if k < LAY - 1:
                q_prev = v * inv
                upp[k, rows, :] = q_prev
                head, conduct, v_prev, flux_prev = head_n, conduct_n, v, flux
        return carry

    lax.fori_loop(0, RX // BLOCK, factor_first, 0)
    lax.fori_loop(0, GROUPS, place, 0)

    for f in range(FIELDS):
        if f < ROOT:
            low_acc = acc[(FIELDS + 1 + f) * 32 : (FIELDS + 2 + f) * 32, :] * (1.0 / 32768.0)
        else:
            low_acc = acc[FIELDS * 32 : FIELDS * 32 + 32, :]
        both = acc[f * 32 : f * 32 + 32, :] + low_acc
        grid[f, 0:32, :] = both[:, :128]
        grid[f, 32:64, :] = both[:, 128:]
    def solve_first(r, carry):
        rows = pl.ds(pl.multiple_of(r * BLOCK, BLOCK), BLOCK)
        prow = pl.ds(pl.multiple_of(r * BLOCK + 8, 8), BLOCK)
        last = rhs[0, rows, :] + (grid[ROOT, rows, :] - grid[0, rows, :]) * rinv[0, rows, :]
        val[0, rows, :] = last
        for k in range(1, LAY):
            here = rhs[k, rows, :]
            if k < ROOT:
                here = here - grid[k, rows, :] * rinv[k, rows, :]
            last = here + low[k, rows, :] * last
            val[k, rows, :] = last
        packed = jnp.zeros((BLOCK, 128), F32)
        for k in range(LAY - 1, -1, -1):
            if k < LAY - 1:
                last = val[k, rows, :] + upp[k, rows, :] * last
            head = pk[0, k, prow, :] + last
            width = par_w[k, rows, :]
            sq, conduct, storage = closures(
                head, par_a[k, rows, :], par_n[k, rows, :], par_e[k, rows, :],
                par_k[k, rows, :], width,
            )
            pk[0, k, prow, :] = head
            pk[1, k, prow, :] = conduct
            stor[k, rows, :] = storage
            rhs[k, rows, :] = 2.0 * width * (sat_old[k, rows, :] - sq * sq)
            packed = jnp.where(pair_b == k, pltpu.roll(head, 2 * k + 1, 1), packed)
            packed = jnp.where(pair_b == k + 32, pltpu.roll(conduct, 2 * k + 65, 1), packed)
        ypack[1, rows, :] = packed
        return carry

    lax.fori_loop(0, RX // BLOCK, solve_first, 0)

    moves = halo_copies(1)
    for move in moves:
        move.start()
    lax.fori_loop(0, LAY, sideways, 0)
    halo_finish(1, moves)

    def solve_second(r, carry):
        rows = pl.ds(pl.multiple_of(r * BLOCK, BLOCK), BLOCK)
        prow = pl.ds(pl.multiple_of(r * BLOCK + 8, 8), BLOCK)
        head, conduct = pk[0, 0, prow, :], pk[1, 0, prow, :]
        v_prev = flux_prev = q_prev = last = None
        for k in range(LAY):
            comb = ycomb[rows, :]
            side_f = jnp.where(ends, pltpu.roll(comb, 127 - 2 * k, 1), 0.0)
            side_g = jnp.where(ends, pltpu.roll(comb, 63 - 2 * k, 1), 0.0)
            target = rhs[k, rows, :] - (lat[k, rows, :] + side_f)
            if k < ROOT:
                target = target - grid[k, rows, :]
            diag = stor[k, rows, :] + (gsum[k, rows, :] + side_g)
            if k < LAY - 1:
                head_n, conduct_n = pk[0, k + 1, prow, :], pk[1, k + 1, prow, :]
                v = 2.0 * (conduct + conduct_n)
                flux = v * (head - head_n + 1.0)
                diag = diag + v
                target = target - flux
            else:
                target = target - 4.0 * conduct
            if k > 0:
                target = target + flux_prev + v_prev * last
                diag = diag + v_prev - v_prev * q_prev
            else:
                target = target + grid[ROOT, rows, :]
            inv = 1.0 / diag
            last = target * inv
            val[k, rows, :] = last
            if k < LAY - 1:
                q_prev = v * inv
                upp[k, rows, :] = q_prev
                head, conduct, v_prev, flux_prev = head_n, conduct_n, v, flux
        numer = denom = jnp.zeros((BLOCK, 128), F32)
        for k in range(LAY - 1, -1, -1):
            if k < LAY - 1:
                last = val[k, rows, :] + upp[k, rows, :] * last
            head = pk[0, k, prow, :] + last
            val[k, rows, :] = head
            if k < ROOT:
                log_s = par_n[k, rows, :] * jnp.log2(
                    par_a[k, rows, :] * jnp.maximum(-head, TINY)
                )
                sat = jnp.exp2(-par_e[k, rows, :] * jnp.log2(1.0 + jnp.exp2(log_s)))
                weight = grid[k, rows, :]
                numer = numer + weight * sat
                denom = denom + weight
        state_ref[rows, :] = numer / jnp.maximum(denom, TINY)
        return carry

    lax.fori_loop(0, RX // BLOCK, solve_second, 0)
    out_copy = pltpu.make_async_copy(val, p_out, out_sem)
    out_copy.start()

    state = jnp.concatenate([state_ref[0:32, :], state_ref[32:64, :]], axis=1)
    s_hi = state.astype(BF16)
    left = state - s_hi.astype(F32)
    s_mid = left.astype(BF16)
    s_low = (left - s_mid.astype(F32)).astype(BF16)
    pieces = jnp.concatenate([s_hi, s_mid, s_low], axis=0)
    iota_r1 = lax.broadcasted_iota(I32, (32, 1024), 0)

    for g in sorted(range(GROUPS), key=lambda w: -WAVES[w]):
        got = lax.dot_general(
            pieces, b_mat[g], (((1,), (0,)), ((), ())), preferred_element_type=F32
        )
        got = got[0:32] + got[32:64] + got[64:96]
        line = jnp.sum(jnp.where(iota_r1 == row_of[g], got, 0.0), axis=0, keepdims=True)
        for j in range(PER):
            back[g * PER + j] = line[:, j * 128 : (j + 1) * 128]
        for target in TARGETS:
            spot = PLACE[target[0]]
            if spot // PER == g:
                pltpu.make_async_remote_copy(
                    back.at[spot], mine.at[me], ret_send, ret_recv,
                    device_id=peer(target), device_id_type=MESH,
                ).start()
    pltpu.make_async_copy(back.at[OWN], mine.at[me], ret_recv).start()
    pltpu.make_async_copy(mine, mine, ret_recv).wait()

    even, other = mine[pl.ds(0, 64, 2), 0, :], mine[pl.ds(1, 64, 2), 0, :]
    low_half = jnp.where(lane < 64, even, pltpu.roll(other, 64, 1))
    high_half = jnp.where(lane < 64, pltpu.roll(even, 64, 1), other)
    s_out[...] = jnp.where(lax.rem(me, 2) == 0, low_half, high_half)

    pltpu.make_async_copy(send.at[0 : PEERS - 1], send.at[0 : PEERS - 1], send_sem).wait()
    pltpu.make_async_copy(mine.at[0 : PEERS - 1], mine.at[0 : PEERS - 1], ret_send).wait()
    out_copy.wait()


def deliver(p_in, s_in, p_out, s_out, held, line, sem_in, sem_out):
    steps = [
        (p_in.at[pl.ds(k, 4)], held.at[pl.ds(k, 4)], p_out.at[pl.ds(k, 4)]) for k in range(0, LAY, 4)
    ]
    steps.append((s_in, line, s_out))
    reads = [
        pltpu.make_async_copy(a, b, sem_in.at[i]) for i, (a, b, _) in enumerate(steps)
    ]
    writes = [
        pltpu.make_async_copy(b, c, sem_out.at[i]) for i, (_, b, c) in enumerate(steps)
    ]
    for read in reads:
        read.start()
    for read, write in zip(reads, writes):
        read.wait()
        write.start()
    for write in writes:
        write.wait()


def on_device(h_old, soil_type, ks_scale, soil_table, clump_brick, clump_cell, root_fraction,
              transpiration, infiltration):
    del clump_brick
    whole = lambda shape, dtype=F32: pltpu.VMEM(shape, dtype)
    cube = whole((LAY, RX, RY))
    dma = pltpu.SemaphoreType.DMA
    vmem = pl.BlockSpec(memory_space=pltpu.VMEM)
    hbm = pl.BlockSpec(memory_space=pl.ANY)
    scratch = [
        cube, whole((LAY, RX, RY), I32), cube,
        whole((1, SLOTS), I32), whole((ROOT, SLOTS)), whole((1, SLOTS)), whole((1, SLOTS)),
        whole((8, 128)), whole((8, SLOTS)), whole((PEERS, 8, 128)), whole((PEERS // 2, 2, 8, 128)),
        cube, cube, cube, cube, cube,
        whole((2, LAY, RX + 16, RY)), cube, cube, cube, cube,
        cube, cube, cube, cube, cube,
        whole((GROUPS, 256, 1024), BF16),
        whole((GROUPS, 1, 1024), I32), whole((FIELDS * 64, 256)), whole((FIELDS, RX, RY)),
        whole((2, RX, 128)), whole((2, 2, RX, 128)), whole((2, 2, 2, LAY, 8, 128)),
        whole((RX, 128)), whole((RX, 128)),
        whole((PEERS // 2, 1, 128)), whole((PEERS, 1, 128)),
        dma((7,)), dma, dma((GROUPS,)), dma((2, 4)), dma((2, 4)), dma, dma, dma,
    ]
    pressure, stress = pl.pallas_call(
        kernel,
        out_shape=(
            jax.ShapeDtypeStruct((LAY, RX, RY), F32),
            jax.ShapeDtypeStruct((PEERS // 2, 128), F32),
        ),
        in_specs=[hbm, hbm, hbm, vmem, hbm, hbm, hbm, hbm],
        out_specs=(hbm, vmem),
        scratch_shapes=scratch,
        compiler_params=pltpu.CompilerParams(
            collective_id=1, has_side_effects=True, vmem_limit_bytes=56 * 1024 * 1024
        ),
        name="step",
    )(
        h_old, soil_type, ks_scale, soil_table, clump_cell.reshape(1, SLOTS), root_fraction,
        transpiration.reshape(1, SLOTS), infiltration.reshape(1, SLOTS),
    )
    pressure, stress = pl.pallas_call(
        deliver,
        out_shape=(
            jax.ShapeDtypeStruct((LAY, RX, RY), F32),
            jax.ShapeDtypeStruct((PEERS // 2, 128), F32),
        ),
        in_specs=[hbm, hbm],
        out_specs=(hbm, hbm),
        scratch_shapes=[cube, whole((PEERS // 2, 128)), dma((6,)), dma((6,))],
        name="deliver",
    )(pressure, stress)
    return pressure, stress.reshape(SLOTS)


def solution(mesh):
    cells = P(None, "bx", "by")
    slots = P(("bx", "by"))
    return jax.shard_map(
        on_device,
        mesh=mesh,
        in_specs=(cells, cells, cells, P(), slots, slots, P(None, ("bx", "by")), slots, slots),
        out_specs=(cells, slots),
        check_vma=False,
    )
```

```python
import itertools

import jax
import jax.numpy as jnp
from jax import lax
from jax.experimental import pallas as pl
from jax.experimental.pallas import tpu as pltpu
from jax.sharding import PartitionSpec as P

MESH = pl.DeviceIdType.MESH
NX, NY = 8, 16
PEERS = NX * NY
LAY, ROOT = 20, 14
RX, RY = 64, 128
SLOTS = RX * RY
FIELDS = ROOT + 1
BLOCK = 32
TINY = 1e-30
F32, BF16, I32 = jnp.float32, jnp.bfloat16, jnp.int32
F8 = jnp.float8_e4m3fn


def ring(d):
    return min(d, 4 - d)


PAIRS = sorted(
    itertools.product(range(4), range(2), range(4), range(2)),
    key=lambda o: (ring(o[0]) + ring(o[2]) + o[3], o[1], ring(o[0])),
)
GROUPS, PER = 8, 8
WAVES = (0, 1, 2, 3, 4, 5, 6, 7)
PLACE = {
    pair: wave * PER + i
    for wave, group in enumerate(WAVES)
    for i, pair in enumerate(PAIRS[group * PER : group * PER + PER])
}
OWN = PLACE[0, 0, 0, 0]
TARGETS = [
    (pair, b)
    for group in WAVES
    for pair in reversed(PAIRS[group * PER : group * PER + PER])
    for b in (1, 0)
    if any(pair) or b
]


def seen_back(pair):
    return PLACE[-pair[0] % 4, pair[1], -pair[2] % 4, pair[3]]


def closures(head, alpha, shape_n, exponent, ks, width):
    log_s = shape_n * jnp.log2(alpha * jnp.maximum(-head, TINY))
    log_b = jnp.log2(1.0 + jnp.exp2(log_s))
    log_w = exponent * (log_s - log_b)
    root = jnp.exp2(-0.5 * exponent * log_b)
    inner = 1.0 - jnp.exp2(log_w)
    conduct = ks * root * (inner * inner)
    storage = 0.4 + 2.0 * width * (shape_n - 1.0) * alpha * jnp.exp2(log_w - log_b)
    return root, conduct, storage


def kernel(
    h_hbm, soil_hbm, ks_hbm, table_ref, cell_hbm, root_hbm, transp_hbm, infil_hbm,
    p_out, s_out,
    h, soil, ks_in, cell, root, transp, infil,
    table, fields1, send, recv,
    par_a, par_n, par_e, par_k, par_w,
    pk, sat_old, stor, lat, gsum,
    rinv, low, upp, rhs, val,
    b_mat, row_of, acc, grid,
    ypack, yrecv, xrecv, ycomb, state_ref,
    back, mine,
    in_sem, send_sem, recv_sem, halo_send, halo_recv, ret_send, ret_recv, out_sem,
):
    bx = lax.axis_index("bx")
    by = lax.axis_index("by")
    me = bx * NY + by

    copies = [
        pltpu.make_async_copy(src, dst, in_sem.at[i])
        for i, (src, dst) in enumerate(
            (
                (root_hbm, root), (transp_hbm, transp), (infil_hbm, infil), (cell_hbm, cell),
                (h_hbm, h), (soil_hbm, soil), (ks_hbm, ks_in),
            )
        )
    ]
    for copy in copies:
        copy.start()

    core = lax.rem(bx, 2)
    cores = (core, 1 - core)
    ys = [lax.rem(bx // 2 + d, 4) * 2 for d in range(4)]
    xs = [lax.rem(by // 4 + d, 4) * 4 for d in range(4)]
    half = lax.rem(by, 2)
    halves = (half, 1 - half)
    upper = lax.rem(by, 4) - half
    zs = (upper, 2 - upper)

    def peer(target):
        (y, c, x, z), b = target
        return ys[y] + cores[c], xs[x] + zs[z] + halves[b]

    barrier = pltpu.get_barrier_semaphore()
    for target in TARGETS:
        pl.semaphore_signal(barrier, inc=1, device_id=peer(target), device_id_type=MESH)

    lane8 = lax.broadcasted_iota(I32, (8, 128), 1)
    sub8 = lax.broadcasted_iota(I32, (8, 128), 0)
    first_half = lane8 < 64

    for copy in copies[:4]:
        copy.wait()
    fields1[0:6, :] = root[8:14, :]
    fields1[6:7, :] = infil[...]
    fields1[7:8, :] = cell[...].astype(F32)

    def pack(q, carry):
        at = pl.ds(pl.multiple_of(q * 128, 128), 128)
        demand = transp[:, at]
        v0 = root[0:8, at] * demand
        v1 = fields1[:, at] * jnp.where(sub8 < 6, demand, 1.0)
        r0 = pltpu.roll(v0, 64, 1)
        r1 = pltpu.roll(v1, 64, 1)
        send[2 * q] = jnp.where(first_half, v0, r1)
        send[2 * q + 1] = jnp.where(first_half, r0, v1)
        return carry

    lax.fori_loop(0, PEERS // 2, pack, 0, unroll=8)

    table[...] = jnp.zeros_like(table)
    table[0:4, 0:12] = table_ref[...]
    for copy in copies[4:]:
        copy.wait()
    t0, t1, t2, t3 = (jnp.broadcast_to(table[i : i + 1, :], (RX, 128)) for i in range(4))
    lane = lax.broadcasted_iota(I32, (RX, 128), 1)

    def first(k, packed):
        kind = soil[k]
        look = lambda t: jnp.take_along_axis(t, kind, axis=1, mode="promise_in_bounds")
        alpha = 4.0 * look(t0)
        shape_n = 1.2 + 2.0 * look(t1)
        ks = 0.75 * look(t2) * ks_in[k]
        width = 0.25 + 0.3 * look(t3)
        exponent = 1.0 - 1.0 / shape_n
        par_a[k], par_n[k], par_e[k], par_k[k], par_w[k] = alpha, shape_n, exponent, ks, width
        head = h[k]
        sq, conduct, storage = closures(head, alpha, shape_n, exponent, ks, width)
        sat_old[k] = sq * sq
        stor[k] = storage
        pk[0, k, 8 : 8 + RX, :] = head
        pk[1, k, 8 : 8 + RX, :] = conduct
        turn = 2 * k + 1
        pair = lane // 2
        packed = jnp.where(pair == k, pltpu.roll(head, turn, 1), packed)
        packed = jnp.where(pair == k + 32, pltpu.roll(conduct, turn + 64, 1), packed)
        return packed

    ypack[0] = lax.fori_loop(0, LAY, first, jnp.zeros((RX, 128), F32))

    pl.semaphore_wait(barrier, PEERS - 1)

    def halo_copies(step):
        up = lax.rem(bx + NX - 1, NX), by
        down = lax.rem(bx + 1, NX), by
        left = bx, lax.rem(by + NY - 1, NY)
        right = bx, lax.rem(by + 1, NY)
        moves = (
            (pk.at[:, :, pl.ds(71, 1), :], xrecv.at[step, 0, :, :, pl.ds(0, 1), :], down),
            (pk.at[:, :, pl.ds(8, 1), :], xrecv.at[step, 1, :, :, pl.ds(7, 1), :], up),
            (ypack.at[step], yrecv.at[step, 0], right),
            (ypack.at[step], yrecv.at[step, 1], left),
        )
        return [
            pltpu.make_async_remote_copy(
                src, dst, halo_send.at[step, i], halo_recv.at[step, i],
                device_id=to, device_id_type=MESH,
            )
            for i, (src, dst, to) in enumerate(moves)
        ]

    odd = lax.rem(lane, 2) == 1
    lane_b = lax.broadcasted_iota(I32, (BLOCK, 128), 1)
    pair_b = lane_b // 2

    def halo_finish(step, moves):
        for move in moves:
            move.wait_recv()
        for move in moves:
            move.wait_send()
        own = ypack[step]
        both = jnp.where(
            odd, pltpu.roll(yrecv[step, 0], 1, 1), pltpu.roll(yrecv[step, 1], 127, 1)
        )
        edge = jnp.logical_or(
            jnp.logical_and(odd, by == 0), jnp.logical_and(jnp.logical_not(odd), by == NY - 1)
        )
        both = jnp.where(edge, -own, both)
        face = pltpu.roll(own + both, 64, 1)
        flow = face * (own - both)
        ycomb[...] = jnp.where(lane < 64, flow, own + both)
        for side, row, off in ((0, 0, bx == 0), (1, 7, bx == NX - 1)):
            tile = pl.ds(side * (RX - 8), 8)
            owned = pl.ds(side * (RX - 8) + 8, 8)
            here = sub8 == row
            for k in range(LAY):
                k_own = pk[1, k, owned, :]
                g = k_own + jnp.where(off, -k_own, xrecv[step, side, 1, k])
                f = g * (pk[0, k, owned, :] - xrecv[step, side, 0, k])
                gsum[k, tile, :] += jnp.where(here, g, 0.0)
                lat[k, tile, :] += jnp.where(here, f, 0.0)

    at_first = lane == 0

    def sideways(k, carry):
        head, conduct = pk[0, k, 8:72, :], pk[1, k, 8:72, :]
        g = jnp.where(at_first, 0.0, conduct + pltpu.roll(conduct, 1, 1))
        f = g * (head - pltpu.roll(head, 1, 1))
        gx = conduct[:-1] + conduct[1:]
        fx = gx * (head[1:] - head[:-1])
        zero = jnp.zeros((1, 128), F32)
        gx0 = jnp.concatenate([zero, gx], axis=0)
        gx1 = jnp.concatenate([gx, zero], axis=0)
        fx0 = jnp.concatenate([zero, fx], axis=0)
        fx1 = jnp.concatenate([fx, zero], axis=0)
        gsum[k] = (g + pltpu.roll(g, 127, 1)) + (gx0 + gx1)
        lat[k] = (f - pltpu.roll(f, 127, 1)) + (fx0 - fx1)
        return carry

    moves = halo_copies(0)
    for move in moves:
        move.start()

    pltpu.make_async_copy(send.at[me], recv.at[OWN, half], recv_sem.at[OWN // PER]).start()
    for target in TARGETS:
        tx, ty = peer(target)
        spot = seen_back(target[0])
        pltpu.make_async_remote_copy(
            send.at[tx * NY + ty], recv.at[spot, half], send_sem, recv_sem.at[spot // PER],
            device_id=(tx, ty), device_id_type=MESH,
        ).start()

    lax.fori_loop(0, LAY, sideways, 0)
    iota_c = lax.broadcasted_iota(I32, (256, 128), 0)
    iota_r = lax.broadcasted_iota(I32, (32, 128), 0)
    acc[...] = jnp.zeros_like(acc)

    def spread_tile(g, j):
        m0, m1 = recv[g * PER + j, 0], recv[g * PER + j, 1]
        v0 = jnp.where(first_half, m0, pltpu.roll(m1, 64, 1))
        v1 = jnp.where(first_half, pltpu.roll(m0, 64, 1), m1)
        at = slice(j * 128, (j + 1) * 128)
        spot = v1[7:8, :].astype(I32)
        brow = spot >> 7
        col = (spot & 127) + ((brow >> 5) << 7)
        brow = brow & 31
        row_of[g, :, at] = brow
        b_mat[g, :, at] = jnp.where(iota_c == col, 1.0, 0.0).astype(BF16)
        hit = iota_r == brow
        spread = lambda line: jnp.where(hit, line, 0.0).astype(BF16)
        fine = lambda line: jnp.where(hit, line, 0.0).astype(F8)
        h0 = v0.astype(BF16).astype(F32)
        h1 = v1.astype(BF16).astype(F32)
        high, low_part = [], []
        for f in range(FIELDS):
            top, whole_v = (h0, v0) if f < 8 else (h1, v1)
            row = slice(f % 8, f % 8 + 1)
            high.append(spread(top[row]))
            if f < ROOT:
                low_part.append(fine(((whole_v - top) * 32768.0)[row]))
        high.append(spread((v1 - h1)[6:7]))
        cols = jnp.where(iota_c == col, 1.0, 0.0).astype(F8)
        return jnp.concatenate(high, axis=0), jnp.concatenate(low_part, axis=0), cols

    def place(g, carry):
        part_of = recv.at[pl.ds(g * PER, PER)]
        pltpu.make_async_copy(part_of, part_of, recv_sem.at[g]).wait()
        for part in range(PER // 2):
            blocks = [spread_tile(g, j) for j in range(part * 2, part * 2 + 2)]
            high, low_part, cols = (jnp.concatenate(b, axis=1) for b in zip(*blocks))
            dims = (((1,), (1,)), ((), ()))
            acc[0 : FIELDS * 32 + 32] += lax.dot_general(
                high, b_mat[g, :, part * 256 : part * 256 + 256], dims, preferred_element_type=F32
            )
            acc[FIELDS * 32 + 32 : FIELDS * 64] += lax.dot_general(
                low_part, cols, dims, preferred_element_type=F32
            )
        return carry

    halo_finish(0, moves)
    ends = jnp.logical_or(lane_b == 0, lane_b == 127)

    def factor_first(r, carry):
        rows = pl.ds(pl.multiple_of(r * BLOCK, BLOCK), BLOCK)
        prow = pl.ds(pl.multiple_of(r * BLOCK + 8, 8), BLOCK)
        head, conduct = pk[0, 0, prow, :], pk[1, 0, prow, :]
        v_prev = flux_prev = q_prev = None
        for k in range(LAY):
            comb = ycomb[rows, :]
            side_f = jnp.where(ends, pltpu.roll(comb, 127 - 2 * k, 1), 0.0)
            side_g = jnp.where(ends, pltpu.roll(comb, 63 - 2 * k, 1), 0.0)
            target = -(lat[k, rows, :] + side_f)
            diag = stor[k, rows, :] + (gsum[k, rows, :] + side_g)
            if k < LAY - 1:
                head_n, conduct_n = pk[0, k + 1, prow, :], pk[1, k + 1, prow, :]
                v = 2.0 * (conduct + conduct_n)
                flux = v * (head - head_n + 1.0)
                diag = diag + v
                target = target - flux
            else:
                target = target - 4.0 * conduct
            if k > 0:
                target = target + flux_prev
                diag = diag + v_prev - v_prev * q_prev
            inv = 1.0 / diag
            rinv[k, rows, :] = inv
            rhs[k, rows, :] = target * inv
            if k > 0:
                low[k, rows, :] = v_prev * inv
            if k < LAY - 1:
                q_prev = v * inv
                upp[k, rows, :] = q_prev
                head, conduct, v_prev, flux_prev = head_n, conduct_n, v, flux
        return carry

    lax.fori_loop(0, RX // BLOCK, factor_first, 0)
    lax.fori_loop(0, GROUPS, place, 0)

    for f in range(FIELDS):
        if f < ROOT:
            low_acc = acc[(FIELDS + 1 + f) * 32 : (FIELDS + 2 + f) * 32, :] * (1.0 / 32768.0)
        else:
            low_acc = acc[FIELDS * 32 : FIELDS * 32 + 32, :]
        both = acc[f * 32 : f * 32 + 32, :] + low_acc
        grid[f, 0:32, :] = both[:, :128]
        grid[f, 32:64, :] = both[:, 128:]
    def solve_first(r, carry):
        rows = pl.ds(pl.multiple_of(r * BLOCK, BLOCK), BLOCK)
        prow = pl.ds(pl.multiple_of(r * BLOCK + 8, 8), BLOCK)
        last = rhs[0, rows, :] + (grid[ROOT, rows, :] - grid[0, rows, :]) * rinv[0, rows, :]
        val[0, rows, :] = last
        for k in range(1, LAY):
            here = rhs[k, rows, :]
            if k < ROOT:
                here = here - grid[k, rows, :] * rinv[k, rows, :]
            last = here + low[k, rows, :] * last
            val[k, rows, :] = last
        packed = jnp.zeros((BLOCK, 128), F32)
        for k in range(LAY - 1, -1, -1):
            if k < LAY - 1:
                last = val[k, rows, :] + upp[k, rows, :] * last
            head = pk[0, k, prow, :] + last
            width = par_w[k, rows, :]
            sq, conduct, storage = closures(
                head, par_a[k, rows, :], par_n[k, rows, :], par_e[k, rows, :],
                par_k[k, rows, :], width,
            )
            pk[0, k, prow, :] = head
            pk[1, k, prow, :] = conduct
            stor[k, rows, :] = storage
            rhs[k, rows, :] = 2.0 * width * (sat_old[k, rows, :] - sq * sq)
            packed = jnp.where(pair_b == k, pltpu.roll(head, 2 * k + 1, 1), packed)
            packed = jnp.where(pair_b == k + 32, pltpu.roll(conduct, 2 * k + 65, 1), packed)
        ypack[1, rows, :] = packed
        return carry

    lax.fori_loop(0, RX // BLOCK, solve_first, 0)

    moves = halo_copies(1)
    for move in moves:
        move.start()
    lax.fori_loop(0, LAY, sideways, 0)
    halo_finish(1, moves)

    def solve_second(r, carry):
        rows = pl.ds(pl.multiple_of(r * BLOCK, BLOCK), BLOCK)
        prow = pl.ds(pl.multiple_of(r * BLOCK + 8, 8), BLOCK)
        head, conduct = pk[0, 0, prow, :], pk[1, 0, prow, :]
        v_prev = flux_prev = q_prev = last = None
        for k in range(LAY):
            comb = ycomb[rows, :]
            side_f = jnp.where(ends, pltpu.roll(comb, 127 - 2 * k, 1), 0.0)
            side_g = jnp.where(ends, pltpu.roll(comb, 63 - 2 * k, 1), 0.0)
            target = rhs[k, rows, :] - (lat[k, rows, :] + side_f)
            if k < ROOT:
                target = target - grid[k, rows, :]
            diag = stor[k, rows, :] + (gsum[k, rows, :] + side_g)
            if k < LAY - 1:
                head_n, conduct_n = pk[0, k + 1, prow, :], pk[1, k + 1, prow, :]
                v = 2.0 * (conduct + conduct_n)
                flux = v * (head - head_n + 1.0)
                diag = diag + v
                target = target - flux
            else:
                target = target - 4.0 * conduct
            if k > 0:
                target = target + flux_prev + v_prev * last
                diag = diag + v_prev - v_prev * q_prev
            else:
                target = target + grid[ROOT, rows, :]
            inv = 1.0 / diag
            last = target * inv
            val[k, rows, :] = last
            if k < LAY - 1:
                q_prev = v * inv
                upp[k, rows, :] = q_prev
                head, conduct, v_prev, flux_prev = head_n, conduct_n, v, flux
        numer = denom = jnp.zeros((BLOCK, 128), F32)
        for k in range(LAY - 1, -1, -1):
            if k < LAY - 1:
                last = val[k, rows, :] + upp[k, rows, :] * last
            head = pk[0, k, prow, :] + last
            val[k, rows, :] = head
            if k < ROOT:
                log_s = par_n[k, rows, :] * jnp.log2(
                    par_a[k, rows, :] * jnp.maximum(-head, TINY)
                )
                sat = jnp.exp2(-par_e[k, rows, :] * jnp.log2(1.0 + jnp.exp2(log_s)))
                weight = grid[k, rows, :]
                numer = numer + weight * sat
                denom = denom + weight
        state_ref[rows, :] = numer / jnp.maximum(denom, TINY)
        return carry

    lax.fori_loop(0, RX // BLOCK, solve_second, 0)
    out_copy = pltpu.make_async_copy(val, p_out, out_sem)
    out_copy.start()

    state = jnp.concatenate([state_ref[0:32, :], state_ref[32:64, :]], axis=1)
    s_hi = state.astype(BF16)
    s_low = (state - s_hi.astype(F32)).astype(BF16)
    pieces = jnp.concatenate([s_hi, s_low], axis=0)
    iota_r1 = lax.broadcasted_iota(I32, (32, 1024), 0)

    for g in sorted(range(GROUPS), key=lambda w: -WAVES[w]):
        got = lax.dot_general(
            pieces, b_mat[g], (((1,), (0,)), ((), ())), preferred_element_type=F32
        )
        got = got[0:32] + got[32:64]
        line = jnp.sum(jnp.where(iota_r1 == row_of[g], got, 0.0), axis=0, keepdims=True)
        for j in range(PER):
            back[g * PER + j] = line[:, j * 128 : (j + 1) * 128]
        for target in TARGETS:
            spot = PLACE[target[0]]
            if spot // PER == g:
                pltpu.make_async_remote_copy(
                    back.at[spot], mine.at[me], ret_send, ret_recv,
                    device_id=peer(target), device_id_type=MESH,
                ).start()
    pltpu.make_async_copy(back.at[OWN], mine.at[me], ret_recv).start()
    pltpu.make_async_copy(mine, mine, ret_recv).wait()

    even, other = mine[pl.ds(0, 64, 2), 0, :], mine[pl.ds(1, 64, 2), 0, :]
    low_half = jnp.where(lane < 64, even, pltpu.roll(other, 64, 1))
    high_half = jnp.where(lane < 64, pltpu.roll(even, 64, 1), other)
    s_out[...] = jnp.where(lax.rem(me, 2) == 0, low_half, high_half)

    pltpu.make_async_copy(send.at[0 : PEERS - 1], send.at[0 : PEERS - 1], send_sem).wait()
    pltpu.make_async_copy(mine.at[0 : PEERS - 1], mine.at[0 : PEERS - 1], ret_send).wait()
    out_copy.wait()


def deliver(p_in, s_in, p_out, s_out, held, line, sem_in, sem_out):
    steps = [
        (p_in.at[pl.ds(k, 4)], held.at[pl.ds(k, 4)], p_out.at[pl.ds(k, 4)]) for k in range(0, LAY, 4)
    ]
    steps.append((s_in, line, s_out))
    reads = [
        pltpu.make_async_copy(a, b, sem_in.at[i]) for i, (a, b, _) in enumerate(steps)
    ]
    writes = [
        pltpu.make_async_copy(b, c, sem_out.at[i]) for i, (_, b, c) in enumerate(steps)
    ]
    for read in reads:
        read.start()
    for read, write in zip(reads, writes):
        read.wait()
        write.start()
    for write in writes:
        write.wait()


def on_device(h_old, soil_type, ks_scale, soil_table, clump_brick, clump_cell, root_fraction,
              transpiration, infiltration):
    del clump_brick
    whole = lambda shape, dtype=F32: pltpu.VMEM(shape, dtype)
    cube = whole((LAY, RX, RY))
    dma = pltpu.SemaphoreType.DMA
    vmem = pl.BlockSpec(memory_space=pltpu.VMEM)
    hbm = pl.BlockSpec(memory_space=pl.ANY)
    scratch = [
        cube, whole((LAY, RX, RY), I32), cube,
        whole((1, SLOTS), I32), whole((ROOT, SLOTS)), whole((1, SLOTS)), whole((1, SLOTS)),
        whole((8, 128)), whole((8, SLOTS)), whole((PEERS, 8, 128)), whole((PEERS // 2, 2, 8, 128)),
        cube, cube, cube, cube, cube,
        whole((2, LAY, RX + 16, RY)), cube, cube, cube, cube,
        cube, cube, cube, cube, cube,
        whole((GROUPS, 256, 1024), BF16),
        whole((GROUPS, 1, 1024), I32), whole((FIELDS * 64, 256)), whole((FIELDS, RX, RY)),
        whole((2, RX, 128)), whole((2, 2, RX, 128)), whole((2, 2, 2, LAY, 8, 128)),
        whole((RX, 128)), whole((RX, 128)),
        whole((PEERS // 2, 1, 128)), whole((PEERS, 1, 128)),
        dma((7,)), dma, dma((GROUPS,)), dma((2, 4)), dma((2, 4)), dma, dma, dma,
    ]
    pressure, stress = pl.pallas_call(
        kernel,
        out_shape=(
            jax.ShapeDtypeStruct((LAY, RX, RY), F32),
            jax.ShapeDtypeStruct((PEERS // 2, 128), F32),
        ),
        in_specs=[hbm, hbm, hbm, vmem, hbm, hbm, hbm, hbm],
        out_specs=(hbm, vmem),
        scratch_shapes=scratch,
        compiler_params=pltpu.CompilerParams(
            collective_id=1, has_side_effects=True, vmem_limit_bytes=56 * 1024 * 1024
        ),
        name="step",
    )(
        h_old, soil_type, ks_scale, soil_table, clump_cell.reshape(1, SLOTS), root_fraction,
        transpiration.reshape(1, SLOTS), infiltration.reshape(1, SLOTS),
    )
    pressure, stress = pl.pallas_call(
        deliver,
        out_shape=(
            jax.ShapeDtypeStruct((LAY, RX, RY), F32),
            jax.ShapeDtypeStruct((PEERS // 2, 128), F32),
        ),
        in_specs=[hbm, hbm],
        out_specs=(hbm, hbm),
        scratch_shapes=[cube, whole((PEERS // 2, 128)), dma((6,)), dma((6,))],
        name="deliver",
    )(pressure, stress)
    return pressure, stress.reshape(SLOTS)


def solution(mesh):
    cells = P(None, "bx", "by")
    slots = P(("bx", "by"))
    return jax.shard_map(
        on_device,
        mesh=mesh,
        in_specs=(cells, cells, cells, P(), slots, slots, P(None, ("bx", "by")), slots, slots),
        out_specs=(cells, slots),
        check_vma=False,
    )
```
